128 devices in a mesh: rep: 4 (over z_hi, core), fsdp: 32 (over y, x, z_lo).
Axes of the slice: x: 4, y: 4, z: 4 (z_hi: 2, z_lo: 2; z = z_hi * 2 + z_lo), core: 2. Of those that a mesh axis runs over, the one named last changes fastest.
Arguments:
- layer_input: bfloat16 [65536, 8192], P(('rep', 'fsdp')), may hold values from -0.1875 to 0.1875
- out_grad: bfloat16 [65536, 512], P(('rep', 'fsdp')), may hold values from -6 to 6
- master: float32 [4, 8192, 512], P('rep', 'fsdp'), may hold values from -0.0625 to 0.0625
- first_moment: float32 [4, 8192, 512], P('rep', 'fsdp'), may hold values from -6 to 6
- second_moment: float32 [4, 8192, 512], P('rep', 'fsdp'), may hold values from 0.1 to 10
- anchor: float32 [8192, 512], P('fsdp'), may hold values from -0.0625 to 0.0625
- outer_moment: float32 [8192, 512], P('fsdp'), may hold values from -0.06 to 0.06
Outputs:
- input_grad: bfloat16 [65536, 8192], P(('rep', 'fsdp'))
- master_out: float32 [4, 8192, 512], P('rep', 'fsdp')
- first_out: float32 [4, 8192, 512], P('rep', 'fsdp')
- second_out: float32 [4, 8192, 512], P('rep', 'fsdp')
- anchor_out: float32 [8192, 512], P('fsdp')
- outer_out: float32 [8192, 512], P('fsdp')
The draws below stay inside these ranges and needn't reach their ends.
All inputs are finite; a program needn't handle non-finite values.
Results may differ from the reference program's by a relative error of at most 0.0049.
Values may be sent and summed in bfloat16 or wider, within the bound.
A program may use at most 128 MiB of HBM per device.

```python
import math
import jax
import jax.numpy as jnp
from jax import lax

D = 8192
VC = 512
REPS = 4
GROUP_TOK = 16384
TOKENS = 65536


def strengthened(entries, own_key, source, target, blocks, factor):
    def block_of(axis_at):
        return (jnp.arange(entries.shape[axis_at]) // (entries.shape[axis_at] // blocks)).reshape((-1,) + (1,) * (entries.ndim - 1 - axis_at))

    one_side = jax.random.permutation(own_key, blocks)[block_of(target)]
    second = (block_of(target) + blocks // 2) % blocks
    return jnp.where((block_of(source) == one_side) | (block_of(source) == second), factor * entries, entries)


def block_levels(stream_key, extent, shards, smallest, high):
    def one(axis_at, shards_of):
        heights = jax.random.uniform(jax.random.fold_in(jax.random.fold_in(stream_key, 6), axis_at), (shards_of,), jnp.float32, smallest / len(shards), high / len(shards))
        return jnp.repeat(jnp.exp(heights), extent[axis_at] // shards_of).reshape((-1,) + (1,) * (len(extent) - axis_at - 1))

    factor_of = one(*shards[0])
    for cut in shards[1:]:
        factor_of = factor_of * one(*cut)
    return factor_of


def centred(rng, dims, scale, most, split=(), dtype=jnp.bfloat16):
    entries = scale * jax.random.normal(rng, dims, jnp.float32)
    if split:
        entries = entries * block_levels(rng, dims, split, -0.22, 0.18)
    return jnp.clip(entries, -most, most).astype(dtype)


def heavy_noise(rng, dims, spread, reach, split, heavy, dtype=jnp.bfloat16):
    drawn = spread * jax.random.normal(rng, dims, jnp.float32)
    if split:
        drawn = drawn * block_levels(rng, dims, split, -0.22, 0.18)
    return jnp.clip(strengthened(drawn, jax.random.fold_in(rng, 3), *heavy), -reach, reach).astype(dtype)


def setup_inputs(seed: int = 0) -> dict:
    seeds = jax.random.split(jax.random.key(seed), 8)
    return {
        "layer_input": heavy_noise(seeds[0], (TOKENS, D), (GROUP_TOK ** -0.5), 0.1875, ((0, 128),), (0, 1, 128, 5.5)),
        "out_grad": centred(seeds[1], (TOKENS, VC), 1.0, 6.0, ((0, 128),)),
        "master": centred(seeds[2], (REPS, D, VC), D ** -0.5, 0.0625, ((0, 4), (1, 32)), jnp.float32),
        "first_moment": centred(seeds[3], (REPS, D, VC), 1.0, 6.0, ((0, 4), (1, 32)), jnp.float32),
        "second_moment": jnp.clip(jnp.exp(math.log(10.0) - 4.6051702 * jax.random.uniform(seeds[4], (REPS, D, VC), jnp.float32) ** block_levels(seeds[4], (REPS, D, VC), ((0, 4), (1, 32)), -0.2, 0.2)), 0.1, 10.0),
        "anchor": centred(seeds[5], (D, VC), D ** -0.5, 0.0625, ((0, 32),), jnp.float32),
        "outer_moment": centred(seeds[6], (D, VC), 0.01, 0.06, ((0, 32),), jnp.float32),
    }


beta_one = 0.9
beta_two = 0.95
bias_one = 1.0 - 0.9 ** 20
bias_two = 1.0 - 0.95 ** 20

def replica_step(layer_rows, grad_rows, master_rep, first_rep, second_rep):
    weights = master_rep.astype(jnp.bfloat16)
    input_rows = jnp.dot(grad_rows, weights.T, preferred_element_type=jnp.float32).astype(jnp.bfloat16)
    gradient = jnp.dot(layer_rows.T, grad_rows, preferred_element_type=jnp.float32)
    first_new = beta_one * first_rep + (1.0 - beta_one) * gradient
    second_new = beta_two * second_rep + (1.0 - beta_two) * gradient * gradient
    update = first_new / bias_one / (jnp.sqrt(second_new / bias_two) + 1e-08)
    inner = master_rep - 0.002 * (update + 0.1 * master_rep)
    return (input_rows, inner, first_new, second_new)

def reference(layer_input, out_grad, master, first_moment, second_moment, anchor, outer_moment):
    layer_split = layer_input.reshape(REPS, GROUP_TOK, D)
    grad_split = out_grad.reshape(REPS, GROUP_TOK, VC)

    def one_rep(items):
        return replica_step(items[0], items[1], items[2], items[3], items[4])
    input_rows, inner, first_out, second_out = lax.map(one_rep, (layer_split, grad_split, master, first_moment, second_moment))
    input_grad = input_rows.reshape(TOKENS, D)
    mean_old = lax.optimization_barrier(jnp.sum(master, axis=0)) / REPS
    delta = anchor - mean_old
    outer_out = 0.9 * outer_moment + delta
    anchor_out = anchor - 0.7 * (0.9 * outer_out + delta)
    master_out = 0.5 * inner + 0.5 * anchor_out[None]
    return (input_grad, master_out, first_out, second_out, anchor_out, outer_out)
```

```python
import functools

import jax
import jax.numpy as jnp
from jax import lax
from jax.experimental import pallas as pl
from jax.experimental.pallas import tpu as pltpu
from jax.sharding import PartitionSpec as P

MESH = pl.DeviceIdType.MESH
BF16 = jnp.bfloat16
F32 = jnp.float32

beta_one = 0.9
beta_two = 0.95
bias_one = 1.0 - 0.9**20
bias_two = 1.0 - 0.95**20

SHARD = 256
COLS = 512
TOK = 512
SIZE = {"y": 4, "x": 4, "z": 2}

PARTS = (
    (0, 176, 96, "yxz"),
    (176, 176, 96, "xyz"),
    (352, 80, 48, "zyx"),
    (432, 80, 48, "zxy"),
)


def ring_order(k):
    high, low = k // 2, k % 2
    return 2 - low + high - 2 * high * low


def offsets_of(dims, k):
    found = {}
    for d in reversed(dims):
        at = k % SIZE[d]
        k = k // SIZE[d]
        found[d] = ring_order(at) if SIZE[d] == 4 else 1 - at
    return found


def count_of(dims):
    total = 1
    for d in dims:
        total *= SIZE[d]
    return total


def slot_of(dims, offsets):
    at = 0
    for d in dims:
        at = at * SIZE[d] + offsets[d]
    return at


def loop(count, body):
    if count == 1:
        body(0)
    else:
        lax.fori_loop(0, count, lambda k, c: (body(k), c)[1], 0)


class Layout:
    def __init__(self):
        self.names, self.shapes = [], []

    def add(self, name, shape):
        self.names.append(name)
        self.shapes.append(shape)


def layout():
    own = Layout()
    own.add("rows", pltpu.VMEM((4, TOK, 8 * SHARD), BF16))
    own.add("grad", pltpu.VMEM((TOK, COLS), BF16))
    own.add("grad_t", pltpu.VMEM((COLS, TOK), BF16))
    own.add("mast", pltpu.VMEM((SHARD, COLS), F32))
    own.add("weight", pltpu.VMEM((32, COLS, SHARD), BF16))
    own.add("product", pltpu.VMEM((32, TOK, SHARD), BF16))
    own.add("total", pltpu.VMEM((SHARD, COLS), F32))
    own.add("in_sem", pltpu.SemaphoreType.DMA((8,)))
    own.add("out_sem", pltpu.SemaphoreType.DMA((33,)))
    for p, (_, n, _, order) in enumerate(PARTS):
        for s in range(3):
            m = count_of(order[s + 1 :])
            kinds, bufs = (4, 3) if order[s] != "z" else (1, 1)
            own.add(f"send{p}{s}", pltpu.VMEM((bufs, m, n, SHARD), BF16))
            own.add(f"recv{p}{s}", pltpu.VMEM((bufs, m, n, SHARD), BF16))
            for what in ("rs", "rr", "gs", "gr"):
                own.add(f"{what}{p}{s}", pltpu.SemaphoreType.DMA((kinds, m)))
    return own


def kernel(names, rows_hbm, grad_hbm, mast_hbm, out_hbm, total_hbm, *refs):
    ref = dict(zip(names, refs))
    rep, fsdp = lax.axis_index("rep"), lax.axis_index("fsdp")
    me = {"y": fsdp // 8, "x": fsdp // 2 % 4, "z": fsdp % 2}

    def neighbour(d, step):
        at = dict(me)
        at[d] = (me[d] + step) % SIZE[d]
        return (rep, (at["y"] * 4 + at["x"]) * 2 + at["z"])

    to = {"+y": neighbour("y", 1), "-y": neighbour("y", 3), "+x": neighbour("x", 1), "-x": neighbour("x", 3), "z": neighbour("z", 1)}

    row_copies = []
    for k in range(4):
        y = (me["y"] + (2, 1, 3, 0)[k]) % 4
        row_copies.append(
            pltpu.make_async_copy(
                rows_hbm.at[:, pl.ds(pl.multiple_of(y * (8 * SHARD), 8 * SHARD), 8 * SHARD)],
                ref["rows"].at[y],
                ref["in_sem"].at[k],
            )
        )
    mast_copy = pltpu.make_async_copy(mast_hbm, ref["mast"], ref["in_sem"].at[4])
    grad_copy = pltpu.make_async_copy(grad_hbm, ref["grad"], ref["in_sem"].at[5])
    mast_copy.start()
    grad_copy.start()
    for copy in row_copies:
        copy.start()

    barrier = pltpu.get_barrier_semaphore()
    for target in to.values():
        pl.semaphore_signal(barrier, inc=1, device_id=target, device_id_type=MESH)

    mast_copy.wait()
    ref["weight"][0] = jnp.transpose(ref["mast"][...]).astype(BF16)
    pl.semaphore_wait(barrier, len(to))

    def remote(src, dst, send_sem, recv_sem, target):
        return pltpu.make_async_remote_copy(
            src_ref=src, dst_ref=dst, send_sem=send_sem, recv_sem=recv_sem, device_id=target, device_id_type=MESH
        )

    def weight_at(offsets, first, count):
        return ref["weight"].at[slot_of("yxz", offsets), pl.ds(first, count)]

    def gather_dims(p, s):
        return PARTS[p][3][s + 1 :]

    def gather_copy(p, s, inner, kind):
        first, n, low, order = PARTS[p]
        d, dims = order[s], gather_dims(p, s)
        base = {"y": 0, "x": 0, "z": 0, **inner}
        slot = slot_of(dims, inner)
        if d == "z":
            src, dst, a, c, target = 0, 1, first, n, to["z"]
        else:
            src, dst, a, c, target = (
                (0, 3, first, n, to["+" + d]),
                (0, 1, first, n, to["-" + d]),
                (3, 2, first, low, to["+" + d]),
                (1, 2, first + low, n - low, to["-" + d]),
            )[kind]
        return remote(
            weight_at({**base, d: src}, a, c),
            weight_at({**base, d: dst}, a, c),
            ref[f"gs{p}{s}"].at[kind, slot],
            ref[f"gr{p}{s}"].at[kind, slot],
            target,
        )

    def gather_send(p, s, inner):
        for kind in range(1 if PARTS[p][3][s] == "z" else 2):
            gather_copy(p, s, inner, kind).start()

    def gather_pass(p, s, inner):
        for kind in (0, 1):
            gather_copy(p, s, inner, kind).wait_recv()
            gather_copy(p, s, inner, kind + 2).start()

    def gather_far(p, s, inner):
        for kind in (2, 3):
            gather_copy(p, s, inner, kind).wait_recv()

    def own_tile(p, o):
        first, n = PARTS[p][:2]
        y, x, z = [(me[d] + o[d]) % SIZE[d] for d in "yxz"]
        column = pl.multiple_of((x * 2 + z) * SHARD, SHARD)
        return jnp.dot(
            ref["grad_t"][first : first + n, :],
            ref["rows"][y, :, pl.ds(column, SHARD)],
            preferred_element_type=F32,
        )

    def reduce_copy(p, s, inner, kind):
        _, n, low, order = PARTS[p]
        d = order[s]
        slot = slot_of(order[s + 1 :], inner)
        if d == "z":
            buf, a, c, target = 0, 0, n, to["z"]
        else:
            buf, a, c, target = (
                (0, 0, low, to["+" + d]),
                (0, low, n - low, to["-" + d]),
                (1, 0, n, to["+" + d]),
                (2, 0, n, to["-" + d]),
            )[kind]
        return remote(
            ref[f"send{p}{s}"].at[buf, slot, pl.ds(a, c)],
            ref[f"recv{p}{s}"].at[buf, slot, pl.ds(a, c)],
            ref[f"rs{p}{s}"].at[kind, slot],
            ref[f"rr{p}{s}"].at[kind, slot],
            target,
        )

    def summed(p, s, offsets):
        if s == 0:
            return own_tile(p, offsets)
        d = PARTS[p][3][s - 1]
        dims = PARTS[p][3][s:]
        inner = {e: offsets[e] for e in dims}
        value = summed(p, s - 1, {**offsets, d: 0})
        slot = slot_of(dims, inner)
        for kind, buf in ((0, 0),) if d == "z" else ((2, 1), (3, 2)):
            reduce_copy(p, s - 1, inner, kind).wait_recv()
            value = value + ref[f"recv{p}{s - 1}"][buf, slot].astype(F32)
        return value

    def reduce_far(p, s, inner):
        d = PARTS[p][3][s]
        value = summed(p, s, {**inner, d: 1 if d == "z" else 2})
        ref[f"send{p}{s}"][0, slot_of(PARTS[p][3][s + 1 :], inner)] = value.astype(BF16)
        for kind in range(1 if d == "z" else 2):
            reduce_copy(p, s, inner, kind).start()

    def reduce_near(p, s, inner):
        _, n, low, order = PARTS[p]
        d = order[s]
        slot = slot_of(order[s + 1 :], inner)
        for kind, offset, buf, a, c in ((0, 1, 1, 0, low), (1, 3, 2, low, n - low)):
            value = summed(p, s, {**inner, d: offset})
            reduce_copy(p, s, inner, kind).wait_recv()
            other = ref[f"recv{p}{s}"][0, slot, a : a + c].astype(F32)
            send = ref[f"send{p}{s}"]
            if kind == 0:
                send[buf, slot, :low] = (value[:low] + other).astype(BF16)
                send[buf, slot, low:] = value[low:].astype(BF16)
            else:
                send[buf, slot, :low] = value[:low].astype(BF16)
                send[buf, slot, low:] = (value[low:] + other).astype(BF16)
            reduce_copy(p, s, inner, kind + 2).start()

    def each(p, s, body, first=0, last=None):
        dims = PARTS[p][3][s + 1 :]
        count = count_of(dims)
        last = count if last is None else last
        loop(last - first, lambda k: body(p, s, offsets_of(dims, k + first)))

    def gather_inner(p, s, skip_own=True):
        dims = gather_dims(p, s)
        return dims, count_of(dims)

    def each_gather(p, s, body, first=0, last=None):
        dims = gather_dims(p, s)
        count = count_of(dims)
        last = count if last is None else last

        def step(k):
            inner, at = {}, k + first
            for d in reversed(dims):
                inner[d] = at % SIZE[d]
                at = at // SIZE[d]
            body(p, s, inner)

        loop(last - first, step)

    own = {"y": 0, "x": 0, "z": 0}

    def own_inner(p, s):
        return {d: 0 for d in gather_dims(p, s)}

    for p, s in ((0, 2), (1, 2), (2, 2), (3, 2), (2, 1), (3, 1), (0, 1), (1, 1), (0, 0), (1, 0), (2, 0), (3, 0)):
        gather_send(p, s, own_inner(p, s))

    grad_copy.wait()
    ref["grad_t"][...] = jnp.transpose(ref["grad"][...].astype(F32)).astype(BF16)
    for copy in row_copies:
        copy.wait()

    each(0, 0, reduce_far)
    each(1, 0, reduce_far)
    each(2, 0, reduce_far, 0, 8)
    each(3, 0, reduce_far, 0, 8)

    for p in (0, 1):
        gather_copy(p, 2, {}, 0).wait_recv()
        gather_send(p, 1, {"z": 1})
    for p in (2, 3):
        gather_pass(p, 2, {})

    each(2, 0, reduce_far, 8, 16)
    each(3, 0, reduce_far, 8, 16)
    each(0, 0, reduce_near)
    each(1, 0, reduce_near)

    def pass_then_send(p, s, inner):
        gather_pass(p, s, inner)
        d = PARTS[p][3][s]
        for offset in (1, 3):
            gather_send(p, s - 1, {**inner, d: offset})

    def far_then_send(p, s, inner):
        gather_far(p, s, inner)
        gather_send(p, s - 1, {**inner, PARTS[p][3][s]: 2})

    for p in (0, 1):
        gather_send(p, 0, {PARTS[p][3][1]: 0, "z": 1})
    for p in (0, 1):
        for z in (0, 1):
            pass_then_send(p, 1, {"z": z})
    for p in (2, 3):
        d = PARTS[p][3][2]
        for offset in (1, 3):
            gather_send(p, 1, {d: offset})
            gather_send(p, 0, {d: offset, PARTS[p][3][1]: 0})
        gather_far(p, 2, {})
        gather_send(p, 1, {d: 2})
        gather_send(p, 0, {d: 2, PARTS[p][3][1]: 0})
    for p in (0, 1):
        for z in (0, 1):
            far_then_send(p, 1, {"z": z})

    for p in (2, 3):
        each(p, 1, reduce_far)
    for p in (2, 3):
        each(p, 1, reduce_near)
    for p in (2, 3):
        each_gather(p, 1, pass_then_send)

    for p in (0, 1):
        each(p, 1, reduce_far)
    for p in (2, 3):
        each(p, 2, reduce_far)
    for p in (0, 1):
        each(p, 1, reduce_near)
    for p in (2, 3):
        each(p, 2, reduce_near)
    for p in (2, 3):
        each_gather(p, 1, far_then_send)
    for p in (0, 1):
        each(p, 2, reduce_far)
    for p in (0, 1, 2, 3):
        first, n = PARTS[p][:2]
        value = summed(p, 3, dict(own))
        ref["grad_sum"][first : first + n, :] = value
    ref["total"][...] = jnp.transpose(ref["grad_sum"][...])
    total_copy = pltpu.make_async_copy(ref["total"], total_hbm, ref["out_sem"].at[32])
    total_copy.start()

    for p in (0, 1):
        each_gather(p, 0, gather_pass)

    def product_copy(o):
        y, x, z = [(me[d] + o[d]) % SIZE[d] for d in "yxz"]
        column = pl.multiple_of(((y * 4 + x) * 2 + z) * SHARD, SHARD)
        slot = slot_of("yxz", o)
        return pltpu.make_async_copy(ref["product"].at[slot], out_hbm.at[:, pl.ds(column, SHARD)], ref["out_sem"].at[slot])

    def multiply(o):
        slot = slot_of("yxz", o)
        ref["product"][slot] = jnp.dot(ref["grad"][...], ref["weight"][slot], preferred_element_type=F32).astype(BF16)
        product_copy(o).start()

    def near(k):
        return k + k // 2

    loop(9, lambda k: multiply({"y": near(k // 3), "x": near(k % 3), "z": 0}))

    def along_z(o):
        for p in (2, 3):
            gather_copy(p, 0, {"y": o["y"], "x": o["x"]}, 0).wait_recv()

    def near_z(k):
        o = {"y": near(k // 3), "x": near(k % 3), "z": 1}
        along_z(o)
        multiply(o)

    loop(9, near_z)

    def far_x(z):
        def step(k):
            o = {"y": near(k), "x": 2, "z": z}
            gather_far(1, 0, {"y": o["y"], "z": z})
            if z:
                along_z(o)
            multiply(o)

        loop(3, step)

    def far_y(z):
        def step(k):
            o = {"y": 2, "x": near(k), "z": z}
            gather_far(0, 0, {"x": o["x"], "z": z})
            if z:
                along_z(o)
            multiply(o)

        loop(3, step)

    for z in (0, 1):
        far_x(z)
        far_y(z)
    for z in (0, 1):
        o = {"y": 2, "x": 2, "z": z}
        gather_far(0, 0, {"x": 2, "z": z})
        gather_far(1, 0, {"y": 2, "z": z})
        if z:
            along_z(o)
        multiply(o)

    for p in range(4):
        for s in range(3):
            for kind in range(1 if PARTS[p][3][s] == "z" else 4):
                each_gather(p, s, lambda p, s, inner: gather_copy(p, s, inner, kind).wait_send())
                each_gather(p, s, lambda p, s, inner: reduce_copy(p, s, inner, kind).wait_send())
    total_copy.wait()

    def finish(k):
        product_copy({"y": k // 8, "x": k // 2 % 4, "z": k % 2}).wait()

    loop(32, finish)


def exchange(layer_input, out_grad, master_local):
    own = layout()
    own.add("grad_sum", pltpu.VMEM((COLS, SHARD), F32))
    return pl.pallas_call(
        functools.partial(kernel, tuple(own.names)),
        out_shape=(
            jax.ShapeDtypeStruct((TOK, 32 * SHARD), BF16),
            jax.ShapeDtypeStruct((SHARD, COLS), F32),
        ),
        in_specs=[pl.BlockSpec(memory_space=pltpu.HBM)] * 3,
        out_specs=[pl.BlockSpec(memory_space=pltpu.HBM)] * 2,
        scratch_shapes=own.shapes,
        compiler_params=pltpu.CompilerParams(collective_id=0, has_side_effects=True, vmem_limit_bytes=60 << 20),
        cost_estimate=pl.CostEstimate(flops=2 * 2 * TOK * COLS * 32 * SHARD, bytes_accessed=20 << 20, transcendentals=0),
    )(layer_input, out_grad, master_local)


def outer_update(anchor_block, moment_block, summed):
    delta = anchor_block - summed / lax.axis_size("rep")
    outer_new = 0.9 * moment_block + delta
    anchor_new = anchor_block - 0.7 * (0.9 * outer_new + delta)
    return (anchor_new, outer_new)


def on_device(layer_input, out_grad, master, first_moment, second_moment, anchor, outer_moment):
    master_local = master[0]
    summed = lax.psum(master_local, "rep")
    input_grad, gradient = exchange(layer_input, out_grad, master_local)
    first_new = beta_one * first_moment[0] + (1.0 - beta_one) * gradient
    second_new = beta_two * second_moment[0] + (1.0 - beta_two) * gradient * gradient
    update = first_new / bias_one / (jnp.sqrt(second_new / bias_two) + 1e-08)
    inner = master_local - 0.002 * (update + 0.1 * master_local)
    anchor_new, outer_new = outer_update(anchor, outer_moment, summed)
    master_new = 0.5 * inner + 0.5 * anchor_new
    return (input_grad, master_new[None], first_new[None], second_new[None], anchor_new, outer_new)


def solution(mesh):
    return jax.shard_map(
        on_device,
        mesh=mesh,
        in_specs=(
            P(("rep", "fsdp"), None),
            P(("rep", "fsdp"), None),
            P("rep", "fsdp", None),
            P("rep", "fsdp", None),
            P("rep", "fsdp", None),
            P("fsdp", None),
            P("fsdp", None),
        ),
        out_specs=(
            P(("rep", "fsdp"), None),
            P("rep", "fsdp", None),
            P("rep", "fsdp", None),
            P("rep", "fsdp", None),
            P("fsdp", None),
            P("fsdp", None),
        ),
        check_vma=False,
    )
```

```python
import functools

import jax
import jax.numpy as jnp
from jax import lax
from jax.experimental import pallas as pl
from jax.experimental.pallas import tpu as pltpu
from jax.sharding import PartitionSpec as P

MESH = pl.DeviceIdType.MESH
BF16 = jnp.bfloat16
F32 = jnp.float32

beta_one = 0.9
beta_two = 0.95
bias_one = 1.0 - 0.9**20
bias_two = 1.0 - 0.95**20

SHARD = 256
COLS = 512
TOK = 512
SIZE = {"y": 4, "x": 4, "z": 2}
SHARDS = tuple({"y": y, "x": x, "z": z} for y in range(4) for x in range(4) for z in range(2))

PARTS = (
    (0, 176, 96, 80, "yxz"),
    (176, 176, 80, 96, "xyz"),
    (352, 80, 32, 48, "zyx"),
    (432, 80, 48, 32, "zxy"),
)

RATE, DELAY = 47500.0, 2.0
DOT, PRODUCT, ADD, SEND = 0.33, 0.31, 0.0005, 0.03


def count_of(dims):
    total = 1
    for d in dims:
        total *= SIZE[d]
    return total


def slot_of(dims, offsets):
    at = 0
    for d in dims:
        at = at * SIZE[d] + offsets[d]
    return at


def choices(dims):
    found = [{}]
    for d in dims:
        found = [{**o, d: k} for o in found for k in range(SIZE[d])]
    return found


def reduce_token(p, s, inner, kind):
    return ("reduce", p, s, slot_of(PARTS[p][4][s + 1 :], inner), kind)


def gather_token(p, s, inner, kind):
    return ("gather", p, s, slot_of(PARTS[p][4][s + 1 :], inner), kind)


def links_of(d):
    return ("z",) if d == "z" else ("+" + d, "-" + d)


def make_tasks():
    tasks = []

    def add(name, needs, time, sends, rank):
        tasks.append((name, tuple(needs), time + SEND * len(sends), tuple(sends), rank))

    def term_needs(p, s, o):
        order = PARTS[p][4]
        needs = [("dot", slot_of("yxz", o))]
        for t in range(s):
            inner = {e: o[e] for e in order[t + 1 :]}
            needs += [reduce_token(p, t, inner, k) for k in ((0,) if order[t] == "z" else (2, 3))]
        return needs

    for o in SHARDS:
        sends = []
        for p, (_, n, low, _, order) in enumerate(PARTS):
            d, inner = order[0], {e: o[e] for e in order[1:]}
            if d == "z" and o["z"] == 1:
                sends.append(("z", n * 512, reduce_token(p, 0, inner, 0)))
            if d != "z" and o[d] == 2:
                sends.append(("+" + d, low * 512, reduce_token(p, 0, inner, 0)))
                sends.append(("-" + d, (n - low) * 512, reduce_token(p, 0, inner, 1)))
        far = (o["y"] == 2) + (o["x"] == 2)
        add(("dot", slot_of("yxz", o)), [], DOT, sends, 22 - 2 * far - o["z"])
    for p, (_, n, low, glow, order) in enumerate(PARTS):
        for s in range(3):
            d = order[s]
            for inner in choices(order[s + 1 :]):
                o = {**{e: 0 for e in order[:s]}, **inner}
                at = slot_of(order[s + 1 :], inner)
                if s:
                    sizes = (n,) if d == "z" else (low, n - low)
                    sends = [(link, size * 512, reduce_token(p, s, inner, k)) for k, (link, size) in enumerate(zip(links_of(d), sizes))]
                    add(("far", p, s, at), term_needs(p, s, {**o, d: 1 if d == "z" else 2}), ADD * n * s, sends, 10)
                if d != "z":
                    for k, link in enumerate(links_of(d)):
                        needs = term_needs(p, s, {**o, d: 1 + 2 * k}) + [reduce_token(p, s, inner, k)]
                        add(("near", p, s, at, k), needs, ADD * n * (s + 1), [(link, n * 512, reduce_token(p, s, inner, k + 2))], 10)
        add(("final", p), term_needs(p, 3, {"y": 0, "x": 0, "z": 0}), ADD * n * 4, [], 10)
    add(("total",), [("final", p) for p in range(len(PARTS))], 0.5, [], 10)

    arrivals = {slot: [] for slot in range(32)}
    for p, (_, n, _, low, order) in enumerate(PARTS):
        have = {0: ({"y": 0, "x": 0, "z": 0}, [])}
        for s in (2, 1, 0):
            d = order[s]
            rank = 30 if s == 0 else 0
            for o, needs in list(have.values()):
                inner = {e: o[e] for e in order[s + 1 :]}
                at = slot_of(order[s + 1 :], inner)
                token = [gather_token(p, s, inner, k) for k in range(4)]
                add(("send", p, s, at), needs, 0.0, [(link, n * 512, token[k]) for k, link in enumerate(links_of(d))], rank)
                if d == "z":
                    found = {1: [token[0]]}
                else:
                    add(("pass", p, s, at, 0), [token[0]], 0.0, [("+" + d, low * 512, token[2])], rank)
                    add(("pass", p, s, at, 1), [token[1]], 0.0, [("-" + d, (n - low) * 512, token[3])], rank)
                    found = {3: [token[0]], 1: [token[1]], 2: [token[2], token[3]]}
                for k, tokens in found.items():
                    shard = {**o, d: k}
                    have[slot_of("yxz", shard)] = (shard, tokens)
        for slot, (_, tokens) in have.items():
            arrivals[slot] += tokens
    for slot in range(32):
        add(("product", slot), arrivals[slot] + [("dot", k) for k in range(32)], PRODUCT, [], 90)

    add(("sum", 0), [], 0.0, [("core", SHARD * COLS * 2, ("sum", "in", 0))], 1)
    add(("sum", 1), [("sum", "in", 0)], 0.1, [("z", SHARD * COLS * 2, ("sum", "in", 1))], 11)
    add(("sum", 2), [("sum", "in", 1)], 0.1, [("core", SHARD * COLS * 2, ("sum", "in", 2))], 12)
    add(("sum", 3), [("sum", "in", 2)], 0.0, [], 80)
    return tasks


def in_order(tasks):
    now, done, free, order = 0.0, {}, {}, []
    left = sorted(tasks, key=lambda task: task[4])
    while left:
        ready, soonest = None, None
        for task in left:
            if all(token in done for token in task[1]):
                at = max([done[token] for token in task[1]], default=0.0)
                if at <= now:
                    ready = task
                    break
                soonest = at if soonest is None else min(soonest, at)
        if ready is None:
            now = soonest
            continue
        left.remove(ready)
        order.append(ready)
        now += ready[2]
        done[ready[0]] = now
        for link, size, token in ready[3]:
            rate = 12 * RATE if link == "core" else RATE
            free[link] = max(free.get(link, 0.0), now) + size / rate
            done[token] = free[link] + DELAY
    return order


class Layout:
    def __init__(self):
        self.names, self.shapes = [], []

    def add(self, name, shape):
        self.names.append(name)
        self.shapes.append(shape)


def layout():
    own = Layout()
    own.add("grad", pltpu.VMEM((TOK, COLS), BF16))
    own.add("grad_t", pltpu.VMEM((COLS, TOK), BF16))
    own.add("mast", pltpu.VMEM((SHARD, COLS), F32))
    own.add("weight", pltpu.VMEM((32, COLS, SHARD), BF16))
    own.add("term", pltpu.VMEM((32, COLS, SHARD), F32))
    own.add("sum_send", pltpu.VMEM((SHARD // 2, COLS), F32))
    own.add("sum_recv", pltpu.VMEM((2, SHARD // 2, COLS), F32))
    own.add("sum_ss", pltpu.SemaphoreType.DMA((3,)))
    own.add("sum_rs", pltpu.SemaphoreType.DMA((3,)))
    own.add("grad_sum", pltpu.VMEM((COLS, SHARD), F32))
    own.add("in_sem", pltpu.SemaphoreType.DMA((6,)))
    for p, (_, n, _, _, order) in enumerate(PARTS):
        for s in range(3):
            m = count_of(order[s + 1 :])
            kinds, bufs = (4, 3) if order[s] != "z" else (1, 1)
            own.add(f"send{p}{s}", pltpu.VMEM((bufs, m, n, SHARD), BF16))
            own.add(f"recv{p}{s}", pltpu.VMEM((bufs, m, n, SHARD), BF16))
            for what in ("rr", "gr"):
                own.add(f"{what}{p}{s}", pltpu.SemaphoreType.DMA((kinds, m)))
            for what in ("rs", "gs"):
                own.add(f"{what}{p}{s}", pltpu.SemaphoreType.DMA)
    return own


def kernel(names, rows_hbm, grad_hbm, mast_hbm, out_ref, total_ref, sum_ref, *refs):
    ref = dict(zip(names, refs))
    rep, fsdp = lax.axis_index("rep"), lax.axis_index("fsdp")
    me = {"y": fsdp // 8, "x": fsdp // 2 % 4, "z": fsdp % 2}
    core = rep % 2
    place = {d: [(me[d] + k) % SIZE[d] for k in range(SIZE[d])] for d in "yxz"}

    def device(y, x, z):
        return (rep, (y * 4 + x) * 2 + z)

    to = {
        "+y": device(place["y"][1], me["x"], me["z"]),
        "-y": device(place["y"][3], me["x"], me["z"]),
        "+x": device(me["y"], place["x"][1], me["z"]),
        "-x": device(me["y"], place["x"][3], me["z"]),
        "z": device(me["y"], me["x"], place["z"][1]),
        "core": (rep + 1 - 2 * core, fsdp),
        "far": ((rep + 2) % 4, fsdp),
    }

    barrier = pltpu.get_barrier_semaphore()
    for target in to.values():
        pl.semaphore_signal(barrier, inc=1, device_id=target, device_id_type=MESH)

    mast_copy = pltpu.make_async_copy(mast_hbm, ref["mast"], ref["in_sem"].at[4])
    grad_copy = pltpu.make_async_copy(grad_hbm, ref["grad"], ref["in_sem"].at[5])
    row_copies = []
    for k in range(4):
        columns = pl.ds(pl.multiple_of(place["y"][(2, 1, 3, 0)[k]] * (8 * SHARD), 8 * SHARD), 8 * SHARD)
        row_copies.append(pltpu.make_async_copy(rows_hbm.at[:, columns], out_ref.at[:, columns], ref["in_sem"].at[k]))
    for copy in (mast_copy, grad_copy, *row_copies):
        copy.start()

    def columns_of(o):
        y, x, z = [place[d][o[d]] for d in "yxz"]
        return pl.ds(pl.multiple_of(((y * 4 + x) * 2 + z) * SHARD, SHARD), SHARD)

    def remote(src, dst, send_sem, recv_sem, target):
        return pltpu.make_async_remote_copy(
            src_ref=src, dst_ref=dst, send_sem=send_sem, recv_sem=recv_sem, device_id=target, device_id_type=MESH
        )

    half = SHARD // 2
    mine = pl.ds(pl.multiple_of(core * half, half), half)
    other = pl.ds(pl.multiple_of((1 - core) * half, half), half)

    def sum_copy(k):
        src, dst, target = (
            (ref["mast"].at[other], ref["sum_recv"].at[0], to["core"]),
            (ref["sum_send"], ref["sum_recv"].at[1], to["far"]),
            (sum_ref.at[mine], sum_ref.at[mine], to["core"]),
        )[k]
        return remote(src, dst, ref["sum_ss"].at[k], ref["sum_rs"].at[k], target)

    def weight_at(offsets, first, count):
        return ref["weight"].at[slot_of("yxz", offsets), pl.ds(first, count)]

    def gather_copy(p, s, inner, kind):
        first, n, _, low, order = PARTS[p]
        d, dims = order[s], order[s + 1 :]
        base = {"y": 0, "x": 0, "z": 0, **inner}
        if d == "z":
            src, dst, a, c, link = 0, 1, first, n, "z"
        else:
            src, dst, a, c, link = (
                (0, 3, first, n, "+" + d),
                (0, 1, first, n, "-" + d),
                (3, 2, first, low, "+" + d),
                (1, 2, first + low, n - low, "-" + d),
            )[kind]
        return remote(
            weight_at({**base, d: src}, a, c),
            weight_at({**base, d: dst}, a, c),
            ref[f"gs{p}{s}"],
            ref[f"gr{p}{s}"].at[kind, slot_of(dims, inner)],
            to[link],
        )

    def reduce_copy(p, s, inner, kind):
        _, n, low, _, order = PARTS[p]
        d = order[s]
        slot = slot_of(order[s + 1 :], inner)
        if d == "z":
            buf, a, c, link = 0, 0, n, "z"
        else:
            buf, a, c, link = (
                (0, 0, low, "+" + d),
                (0, low, n - low, "-" + d),
                (1, 0, n, "+" + d),
                (2, 0, n, "-" + d),
            )[kind]
        return remote(
            ref[f"send{p}{s}"].at[buf, slot, pl.ds(a, c)],
            ref[f"recv{p}{s}"].at[buf, slot, pl.ds(a, c)],
            ref[f"rs{p}{s}"],
            ref[f"rr{p}{s}"].at[kind, slot],
            to[link],
        )

    def inner_of(p, s, at):
        return choices(PARTS[p][4][s + 1 :])[at]

    waited = set()

    def wait_for(token):
        if token in waited or token[0] not in ("reduce", "gather") and token[1] != "in":
            return
        waited.add(token)
        if token[0] == "sum":
            sum_copy(token[2]).wait_recv()
        else:
            _, p, s, at, kind = token
            (reduce_copy if token[0] == "reduce" else gather_copy)(p, s, inner_of(p, s, at), kind).wait_recv()

    def term(p, s, o):
        first, n, _, _, order = PARTS[p]
        value = ref["term"][slot_of("yxz", o), first : first + n, :]
        for t in range(s):
            slot = slot_of(order[t + 1 :], o)
            for buf in (0,) if order[t] == "z" else (1, 2):
                value = value + ref[f"recv{p}{t}"][buf, slot].astype(F32)
        return value

    def do_dot(slot):
        o = SHARDS[slot]
        value = jnp.dot(ref["grad_t"][...], out_ref[:, columns_of(o)], preferred_element_type=F32)
        for p, (first, n, _, _, order) in enumerate(PARTS):
            d, inner = order[0], {e: o[e] for e in order[1:]}
            piece = value[first : first + n, :]
            if o[d] == (1 if d == "z" else 2):
                ref[f"send{p}0"][0, slot_of(order[1:], inner)] = piece.astype(BF16)
                for kind in range(len(links_of(d))):
                    reduce_copy(p, 0, inner, kind).start()
            else:
                ref["term"][slot, first : first + n, :] = piece

    def do_far(p, s, at):
        order = PARTS[p][4]
        d, inner = order[s], inner_of(p, s, at)
        o = {**{e: 0 for e in order[:s]}, **inner, d: 1 if d == "z" else 2}
        ref[f"send{p}{s}"][0, at] = term(p, s, o).astype(BF16)
        for kind in range(len(links_of(d))):
            reduce_copy(p, s, inner, kind).start()

    def do_near(p, s, at, kind):
        _, n, low, _, order = PARTS[p]
        d, inner = order[s], inner_of(p, s, at)
        value = term(p, s, {**{e: 0 for e in order[:s]}, **inner, d: 1 + 2 * kind})
        send, recv = ref[f"send{p}{s}"], ref[f"recv{p}{s}"]
        for which, (a, b) in enumerate(((0, low), (low, n))):
            piece = value[a:b]
            if which == kind:
                piece = piece + recv[0, at, a:b].astype(F32)
            send[kind + 1, at, a:b] = piece.astype(BF16)
        reduce_copy(p, s, inner, kind + 2).start()

    def do_final(p):
        first, n = PARTS[p][:2]
        ref["grad_sum"][first : first + n, :] = term(p, 3, {"y": 0, "x": 0, "z": 0})

    def do_total():
        total_ref[...] = jnp.transpose(ref["grad_sum"][...])

    def do_send(p, s, at):
        for kind in range(len(links_of(PARTS[p][4][s]))):
            gather_copy(p, s, inner_of(p, s, at), kind).start()

    def do_pass(p, s, at, kind):
        gather_copy(p, s, inner_of(p, s, at), kind + 2).start()

    def do_product(slot):
        value = jnp.dot(ref["grad"][...], ref["weight"][slot], preferred_element_type=F32)
        out_ref[:, columns_of(SHARDS[slot])] = value.astype(BF16)

    def do_sum(k):
        if k == 1:
            ref["sum_send"][...] = ref["mast"][mine, :] + ref["sum_recv"][0]
        if k == 2:
            sum_ref[mine, :] = ref["sum_send"][...] + ref["sum_recv"][1]
        if k < 3:
            sum_copy(k).start()

    steps = {
        "dot": do_dot,
        "far": do_far,
        "near": do_near,
        "final": do_final,
        "total": do_total,
        "send": do_send,
        "pass": do_pass,
        "product": do_product,
        "sum": do_sum,
    }

    mast_copy.wait()
    ref["weight"][0] = jnp.transpose(ref["mast"][...]).astype(BF16)
    pl.semaphore_wait(barrier, len(to))

    loaded = False
    for name, needs, _, _, _ in in_order(make_tasks()):
        if name[0] == "dot" and not loaded:
            loaded = True
            grad_copy.wait()
            ref["grad_t"][...] = jnp.transpose(ref["grad"][...].astype(F32)).astype(BF16)
            for copy in row_copies:
                copy.wait()
        for token in needs:
            wait_for(token)
        with jax.named_scope(name[0]):
            steps[name[0]](*name[1:])

    for p, (first, n, _, _, order) in enumerate(PARTS):
        for s in range(3):
            send = ref[f"send{p}{s}"]
            remote(send, ref[f"recv{p}{s}"], ref[f"rs{p}{s}"], ref[f"rs{p}{s}"], to["z"]).wait_send()
            count = count_of(order[s + 1 :]) * (1 if order[s] == "z" else 3)
            block = ref["weight"].at[pl.ds(0, count), pl.ds(first, n)]
            remote(block, block, ref[f"gs{p}{s}"], ref[f"gs{p}{s}"], to["z"]).wait_send()
    for k in range(3):
        sum_copy(k).wait_send()


def exchange(layer_input, out_grad, master_local):
    own = layout()
    return pl.pallas_call(
        functools.partial(kernel, tuple(own.names)),
        out_shape=(
            pltpu.VMEM((TOK, 32 * SHARD), BF16),
            pltpu.VMEM((SHARD, COLS), F32),
            pltpu.VMEM((SHARD, COLS), F32),
        ),
        in_specs=[pl.BlockSpec(memory_space=pltpu.HBM)] * 3,
        out_specs=[pl.BlockSpec(memory_space=pltpu.VMEM)] * 3,
        scratch_shapes=own.shapes,
        compiler_params=pltpu.CompilerParams(collective_id=0, has_side_effects=True, vmem_limit_bytes=51 << 20),
        cost_estimate=pl.CostEstimate(flops=2 * 2 * TOK * COLS * 32 * SHARD, bytes_accessed=20 << 20, transcendentals=0),
    )(layer_input, out_grad, master_local)


def outer_update(anchor_block, moment_block, summed):
    delta = anchor_block - summed / lax.axis_size("rep")
    outer_new = 0.9 * moment_block + delta
    anchor_new = anchor_block - 0.7 * (0.9 * outer_new + delta)
    return (anchor_new, outer_new)


def on_device(layer_input, out_grad, master, first_moment, second_moment, anchor, outer_moment):
    master_local = master[0]
    input_grad, gradient, summed = exchange(layer_input, out_grad, master_local)
    first_new = beta_one * first_moment[0] + (1.0 - beta_one) * gradient
    second_new = beta_two * second_moment[0] + (1.0 - beta_two) * gradient * gradient
    update = first_new / bias_one / (jnp.sqrt(second_new / bias_two) + 1e-08)
    inner = master_local - 0.002 * (update + 0.1 * master_local)
    anchor_new, outer_new = outer_update(anchor, outer_moment, summed)
    master_new = 0.5 * inner + 0.5 * anchor_new
    return (input_grad, master_new[None], first_new[None], second_new[None], anchor_new, outer_new)


def solution(mesh):
    return jax.shard_map(
        on_device,
        mesh=mesh,
        in_specs=(
            P(("rep", "fsdp"), None),
            P(("rep", "fsdp"), None),
            P("rep", "fsdp", None),
            P("rep", "fsdp", None),
            P("rep", "fsdp", None),
            P("fsdp", None),
            P("fsdp", None),
        ),
        out_specs=(
            P(("rep", "fsdp"), None),
            P("rep", "fsdp", None),
            P("rep", "fsdp", None),
            P("rep", "fsdp", None),
            P("fsdp", None),
            P("fsdp", None),
        ),
        check_vma=False,
    )
```

```python
import functools

import jax
import jax.numpy as jnp
from jax import lax
from jax.experimental import pallas as pl
from jax.experimental.pallas import tpu as pltpu
from jax.sharding import PartitionSpec as P

MESH = pl.DeviceIdType.MESH
BF16 = jnp.bfloat16
F32 = jnp.float32

beta_one = 0.9
beta_two = 0.95
bias_one = 1.0 - 0.9**20
bias_two = 1.0 - 0.95**20

SHARD = 256
COLS = 512
TOK = 512
SIZE = {"y": 4, "x": 4, "z": 2}
SHARDS = tuple({"y": y, "x": x, "z": z} for y in range(4) for x in range(4) for z in range(2))

REDUCE = (
    (0, 176, 96, "yxz", (2, 2, 1)),
    (176, 176, 80, "xyz", (2, 2, 1)),
    (352, 80, 32, "zyx", (4, 2, 1)),
    (432, 80, 48, "zxy", (4, 2, 1)),
)
GATHER = (
    (0, 176, 80, "yxz", (2, 1, 1)),
    (176, 176, 96, "xyz", (2, 1, 1)),
    (352, 80, 48, "zyx", (4, 1, 1)),
    (432, 80, 32, "zxy", (4, 1, 1)),
)

RATE, MESSAGE, DELAY = 48500.0, 0.08, 1.5
DOT, PRODUCT, ADD, SEND = 0.40, 0.38, 0.0005, 0.02
AHEAD = 6.0


def count_of(dims):
    total = 1
    for d in dims:
        total *= SIZE[d]
    return total


def slot_of(dims, offsets):
    at = 0
    for d in dims:
        at = at * SIZE[d] + offsets[d]
    return at


def choices(dims):
    found = [{}]
    for d in dims:
        found = [{**o, d: k} for o in found for k in range(SIZE[d])]
    return found


def links_of(d):
    return ("z",) if d == "z" else ("+" + d, "-" + d)


def groups_of(parts, p, s):
    _, _, _, order, together = parts[p]
    inner = choices(order[s + 1 :])
    return [inner[k : k + together[s]] for k in range(0, len(inner), together[s])]


def block_of(p, s, buf, slot):
    order = REDUCE[p][3]
    sizes = [count_of(order[t + 1 :]) * (1 if order[t] == "z" else 3) for t in range(s)]
    return sum(sizes) + buf * count_of(order[s + 1 :]) + slot


def group_with(parts, p, s, o):
    _, _, _, order, together = parts[p]
    return slot_of(order[s + 1 :], o) // together[s]


def make_tasks():
    tasks = []

    def add(name, needs, time, sends, rank):
        tasks.append((name, tuple(dict.fromkeys(needs)), time + SEND * len(sends), tuple(sends), rank))

    def term_needs(p, s, o):
        order = REDUCE[p][3]
        needs = [("dot", slot_of("yxz", o))]
        for t in range(s):
            needs.append(("reduce", p, t, group_with(REDUCE, p, t, o), 0 if order[t] == "z" else 1))
        return needs

    for o in SHARDS:
        far = (o["y"] == 2) + (o["x"] == 2)
        add(("dot", slot_of("yxz", o)), [], DOT, [], 22 - 2 * far - o["z"])
    for p, (_, n, low, order, together) in enumerate(REDUCE):
        for s in range(3):
            d, g = order[s], together[s]
            for at, group in enumerate(groups_of(REDUCE, p, s)):
                zero = {e: 0 for e in order[:s]}
                sizes = (n,) if d == "z" else (low, n - low)
                sends = [(link, g * size * 512, ("reduce", p, s, at, 0)) for link, size in zip(links_of(d), sizes)]
                needs = [t for o in group for t in term_needs(p, s, {**zero, **o, d: 1 if d == "z" else 2})]
                add(("far", p, s, at), needs, ADD * n * s * g, sends, 10)
                if d != "z":
                    needs = [t for o in group for k in (1, 3) for t in term_needs(p, s, {**zero, **o, d: k})] + [("reduce", p, s, at, 0)]
                    sends = [(link, g * n * 512, ("reduce", p, s, at, 1)) for link in links_of(d)]
                    add(("near", p, s, at), needs, ADD * n * (s + 1) * g * 2, sends, 10)
        add(("final", p), term_needs(p, 3, {"y": 0, "x": 0, "z": 0}), ADD * n * 4, [], 10)

    arrivals = {slot: [] for slot in range(32)}
    for p, (_, n, low, order, together) in enumerate(GATHER):
        have = {0: []}
        for s in (2, 1, 0):
            d, g = order[s], together[s]
            rank = 30 if s == 0 else 0
            zero = {e: 0 for e in order[: s + 1]}
            new = dict(have)
            for at, group in enumerate(groups_of(GATHER, p, s)):
                needs = [t for o in group for t in have[slot_of("yxz", {**zero, **o})]]
                token = [("gather", p, s, at, k) for k in range(2)]
                add(("send", p, s, at), needs, 0.0, [(link, g * n * 512, token[0]) for link in links_of(d)], rank)
                found = {1: [token[0]]}
                if d != "z":
                    sends = [("+" + d, g * low * 512, token[1]), ("-" + d, g * (n - low) * 512, token[1])]
                    add(("pass", p, s, at), [token[0]], 0.0, sends, rank)
                    found = {3: [token[0]], 1: [token[0]], 2: [token[1]]}
                for k, tokens in found.items():
                    for o in group:
                        new[slot_of("yxz", {**zero, **o, d: k})] = tokens
            have = new
        for slot, tokens in have.items():
            arrivals[slot] += tokens
    for slot in range(32):
        add(("product", slot), arrivals[slot] + [("dot", k) for k in range(32)], PRODUCT, [], 90)

    add(("sum", 0), [], 0.0, [("core", SHARD * COLS * 2, ("sum", "in", 0))], 1)
    add(("sum", 1), [("sum", "in", 0)], 0.1, [("z", SHARD * COLS * 2, ("sum", "in", 1))], 11)
    add(("sum", 2), [("sum", "in", 1)], 0.1, [("core", SHARD * COLS * 2, ("sum", "in", 2))], 12)
    add(("update",), [("sum", "in", 2)] + [("final", p) for p in range(len(REDUCE))], 1.0, [], 80)
    return tasks


def in_order(tasks):
    now, done, free, order = 0.0, {}, {}, []
    left = sorted(tasks, key=lambda task: task[4])
    while left:
        ready, soonest = None, None
        for task in left:
            if task[4] == 30 and any(free.get(link, 0.0) > now + AHEAD for link, _, _ in task[3]):
                at = max(free.get(link, 0.0) - AHEAD for link, _, _ in task[3])
                soonest = at if soonest is None else min(soonest, at)
            elif all(token in done for token in task[1]):
                at = max([done[token] for token in task[1]], default=0.0)
                if at <= now:
                    ready = task
                    break
                soonest = at if soonest is None else min(soonest, at)
        if ready is None:
            now = soonest
            continue
        left.remove(ready)
        order.append(ready)
        now += ready[2]
        done[ready[0]] = now
        for link, size, token in ready[3]:
            rate = 12 * RATE if link == "core" else RATE
            free[link] = max(free.get(link, 0.0), now) + size / rate + MESSAGE
            done[token] = max(done.get(token, 0.0), free[link] + DELAY)
    return order


class Layout:
    def __init__(self):
        self.names, self.shapes = [], []

    def add(self, name, shape):
        self.names.append(name)
        self.shapes.append(shape)


def layout():
    own = Layout()
    own.add("grad", pltpu.VMEM((TOK, COLS), BF16))
    own.add("grad_t", pltpu.VMEM((COLS, TOK), BF16))
    own.add("mast", pltpu.VMEM((SHARD, COLS), F32))
    own.add("weight", pltpu.VMEM((4, 4, 2, COLS, SHARD), BF16))
    own.add("term", pltpu.VMEM((32, COLS, SHARD), F32))
    own.add("sum_send", pltpu.VMEM((SHARD // 2, COLS), F32))
    own.add("sum_recv", pltpu.VMEM((2, SHARD // 2, COLS), F32))
    own.add("sum", pltpu.VMEM((SHARD, COLS), F32))
    own.add("sum_ss", pltpu.SemaphoreType.DMA((3,)))
    own.add("sum_rs", pltpu.SemaphoreType.DMA((3,)))
    own.add("grad_sum", pltpu.VMEM((COLS, SHARD), F32))
    own.add("state", pltpu.VMEM((4, SHARD, COLS), F32))
    own.add("in_sem", pltpu.SemaphoreType.DMA((7,)))
    for p, (_, n, _, _, _) in enumerate(REDUCE):
        own.add(f"send{p}", pltpu.VMEM((31, n, SHARD), BF16))
        own.add(f"recv{p}", pltpu.VMEM((31, n, SHARD), BF16))
    for parts, one, two in ((REDUCE, "rs", "rr"), (GATHER, "gs", "gr")):
        for p in range(len(parts)):
            own.add(f"{one}{p}", pltpu.SemaphoreType.DMA)
            for s in range(3):
                own.add(f"{two}{p}{s}", pltpu.SemaphoreType.DMA((len(links_of(parts[p][3][s])), len(groups_of(parts, p, s)))))
    return own


def kernel(names, rows_hbm, grad_hbm, mast_hbm, first_hbm, second_hbm, anchor_hbm, outer_hbm, out_ref, *refs):
    new_master, new_first, new_second, new_anchor, new_outer = refs[:5]
    refs = refs[5:]
    ref = dict(zip(names, refs))
    rep, fsdp = lax.axis_index("rep"), lax.axis_index("fsdp")
    me = {"y": fsdp // 8, "x": fsdp // 2 % 4, "z": fsdp % 2}
    core = rep % 2
    place = {d: [(me[d] + k) % SIZE[d] for k in range(SIZE[d])] for d in "yxz"}

    def device(y, x, z):
        return (rep, (y * 4 + x) * 2 + z)

    to = {
        "+y": device(place["y"][1], me["x"], me["z"]),
        "-y": device(place["y"][3], me["x"], me["z"]),
        "+x": device(me["y"], place["x"][1], me["z"]),
        "-x": device(me["y"], place["x"][3], me["z"]),
        "z": device(me["y"], me["x"], place["z"][1]),
        "core": (rep + 1 - 2 * core, fsdp),
        "far": ((rep + 2) % 4, fsdp),
    }

    barrier = pltpu.get_barrier_semaphore()
    for target in to.values():
        pl.semaphore_signal(barrier, inc=1, device_id=target, device_id_type=MESH)

    mast_copy = pltpu.make_async_copy(mast_hbm, ref["mast"], ref["in_sem"].at[4])
    grad_copy = pltpu.make_async_copy(grad_hbm, ref["grad"], ref["in_sem"].at[5])
    row_copies = []
    for k in range(4):
        columns = pl.ds(pl.multiple_of(place["y"][(2, 1, 3, 0)[k]] * (8 * SHARD), 8 * SHARD), 8 * SHARD)
        row_copies.append(pltpu.make_async_copy(rows_hbm.at[:, columns], out_ref.at[:, columns], ref["in_sem"].at[k]))
    state_copies = []
    for k, hbm in enumerate((first_hbm, second_hbm, anchor_hbm, outer_hbm)):
        state_copies.append(pltpu.make_async_copy(hbm, ref["state"].at[k], ref["in_sem"].at[6]))
    mast_copy.start()
    grad_copy.start()

    def columns_of(o):
        y, x, z = [place[d][o[d]] for d in "yxz"]
        return pl.ds(pl.multiple_of(((y * 4 + x) * 2 + z) * SHARD, SHARD), SHARD)

    def remote(src, dst, send_sem, recv_sem, target):
        return pltpu.make_async_remote_copy(
            src_ref=src, dst_ref=dst, send_sem=send_sem, recv_sem=recv_sem, device_id=target, device_id_type=MESH
        )

    half = SHARD // 2
    mine = pl.ds(pl.multiple_of(core * half, half), half)
    other = pl.ds(pl.multiple_of((1 - core) * half, half), half)

    def sum_copy(k):
        src, dst, target = (
            (ref["mast"].at[other], ref["sum_recv"].at[0], to["core"]),
            (ref["sum_send"], ref["sum_recv"].at[1], to["far"]),
            (ref["sum"].at[mine], ref["sum"].at[mine], to["core"]),
        )[k]
        return remote(src, dst, ref["sum_ss"].at[k], ref["sum_rs"].at[k], target)

    def weight_at(d, at, group, first, count):
        index = []
        for e in "yxz":
            if e == d:
                index.append(at)
            elif e in group[0] and group[0][e] != group[-1][e]:
                index.append(pl.ds(group[0][e], len(group)))
            else:
                index.append(group[0].get(e, 0))
        return ref["weight"].at[(*index, pl.ds(first, count))]

    def gather_copy(p, s, at, kind):
        first, n, low, order, _ = GATHER[p]
        d = order[s]
        if d == "z":
            src, dst, a, c, link = 0, 1, first, n, "z"
        else:
            src, dst, a, c, link = (
                (0, 3, first, n, "+" + d),
                (0, 1, first, n, "-" + d),
                (3, 2, first, low, "+" + d),
                (1, 2, first + low, n - low, "-" + d),
            )[kind]
        group = groups_of(GATHER, p, s)[at]
        return remote(
            weight_at(d, src, group, a, c),
            weight_at(d, dst, group, a, c),
            ref[f"gs{p}"],
            ref[f"gr{p}{s}"].at[kind // 2, at],
            to[link],
        )

    def reduce_copy(p, s, at, kind):
        _, n, low, order, together = REDUCE[p]
        d = order[s]
        if d == "z":
            buf, a, c, link = 0, 0, n, "z"
        else:
            buf, a, c, link = (
                (0, 0, low, "+" + d),
                (0, low, n - low, "-" + d),
                (1, 0, n, "+" + d),
                (2, 0, n, "-" + d),
            )[kind]
        slots = pl.ds(block_of(p, s, buf, at * together[s]), together[s])
        return remote(
            ref[f"send{p}"].at[slots, pl.ds(a, c)],
            ref[f"recv{p}"].at[slots, pl.ds(a, c)],
            ref[f"rs{p}"],
            ref[f"rr{p}{s}"].at[kind // 2, at],
            to[link],
        )

    def gather_wait(p, s, at, phase):
        first, n, _, order, _ = GATHER[p]
        d, group = order[s], groups_of(GATHER, p, s)[at]
        where = 1 if d == "z" else 2 if phase else pl.ds(0, 2)
        block, sem = weight_at(d, where, group, first, n), ref[f"gr{p}{s}"].at[phase, at]
        remote(block, block, sem, sem, to["z"]).wait_recv()

    def reduce_wait(p, s, at, phase):
        _, n, _, order, together = REDUCE[p]
        g, sem = together[s], ref[f"rr{p}{s}"].at[phase, at]
        count = 2 * g if phase else g
        block = ref[f"recv{p}"].at[pl.ds(block_of(p, s, phase, at * g), count)]
        remote(block, block, sem, sem, to["z"]).wait_recv()

    waited = set()

    def wait_for(token):
        if token in waited or (token[0] not in ("reduce", "gather") and "in" not in token):
            return
        waited.add(token)
        if token[0] == "sum":
            sum_copy(token[2]).wait_recv()
        else:
            (reduce_wait if token[0] == "reduce" else gather_wait)(*token[1:])

    def term(p, s, o):
        first, n, _, order, _ = REDUCE[p]
        value = ref["term"][slot_of("yxz", o), first : first + n, :]
        for t in range(s):
            slot = slot_of(order[t + 1 :], o)
            for buf in (0,) if order[t] == "z" else (1, 2):
                value = value + ref[f"recv{p}"][block_of(p, t, buf, slot)].astype(F32)
        return value

    def do_dot(slot):
        o = SHARDS[slot]
        value = jnp.dot(ref["grad_t"][...], out_ref[:, columns_of(o)], preferred_element_type=F32)
        for p, (first, n, _, order, _) in enumerate(REDUCE):
            d = order[0]
            piece = value[first : first + n, :]
            if o[d] == (1 if d == "z" else 2):
                ref[f"send{p}"][slot_of(order[1:], o)] = piece.astype(BF16)
            else:
                ref["term"][slot, first : first + n, :] = piece

    def do_far(p, s, at):
        order = REDUCE[p][3]
        d = order[s]
        for inner in groups_of(REDUCE, p, s)[at] if s else ():
            o = {**{e: 0 for e in order[:s]}, **inner, d: 1 if d == "z" else 2}
            ref[f"send{p}"][block_of(p, s, 0, slot_of(order[s + 1 :], inner))] = term(p, s, o).astype(BF16)
        for kind in range(len(links_of(d))):
            reduce_copy(p, s, at, kind).start()

    def do_near(p, s, at):
        _, n, low, order, _ = REDUCE[p]
        send, recv = ref[f"send{p}"], ref[f"recv{p}"]
        for kind in (0, 1):
            for inner in groups_of(REDUCE, p, s)[at]:
                value = term(p, s, {**{e: 0 for e in order[:s]}, **inner, order[s]: 1 + 2 * kind})
                slot = slot_of(order[s + 1 :], inner)
                came, goes = block_of(p, s, 0, slot), block_of(p, s, kind + 1, slot)
                for which, (a, b) in enumerate(((0, low), (low, n))):
                    piece = value[a:b]
                    if which == kind:
                        piece = piece + recv[came, a:b].astype(F32)
                    send[goes, a:b] = piece.astype(BF16)
            reduce_copy(p, s, at, kind + 2).start()

    def do_final(p):
        first, n = REDUCE[p][:2]
        ref["grad_sum"][first : first + n, :] = term(p, 3, {"y": 0, "x": 0, "z": 0})

    def do_update():
        pltpu.make_async_copy(ref["state"], ref["state"], ref["in_sem"].at[6]).wait()

        gradient_t = ref["grad_sum"]
        for k in range(2):
            rows = slice(k * 128, k * 128 + 128)
            gradient = jnp.transpose(gradient_t[:, rows])
            master = ref["mast"][rows, :]
            first_new = beta_one * ref["state"][0, rows, :] + (1.0 - beta_one) * gradient
            second_new = beta_two * ref["state"][1, rows, :] + (1.0 - beta_two) * gradient * gradient
            update = first_new / bias_one / (jnp.sqrt(second_new / bias_two) + 1e-08)
            inner = master - 0.002 * (update + 0.1 * master)
            anchor = ref["state"][2, rows, :]
            delta = anchor - ref["sum"][rows, :] / 4.0
            outer_new = 0.9 * ref["state"][3, rows, :] + delta
            anchor_new = anchor - 0.7 * (0.9 * outer_new + delta)
            new_first[rows, :] = first_new
            new_second[rows, :] = second_new
            new_outer[rows, :] = outer_new
            new_anchor[rows, :] = anchor_new
            new_master[rows, :] = 0.5 * inner + 0.5 * anchor_new

    def do_send(p, s, at):
        for kind in range(len(links_of(GATHER[p][3][s]))):
            gather_copy(p, s, at, kind).start()

    def do_pass(p, s, at):
        gather_copy(p, s, at, 2).start()
        gather_copy(p, s, at, 3).start()

    def do_product(slot):
        value = jnp.dot(ref["grad"][...], ref["weight"][tuple(SHARDS[slot].values())], preferred_element_type=F32)
        out_ref[:, columns_of(SHARDS[slot])] = value.astype(BF16)

    def do_sum(k):
        if k == 1:
            ref["sum_send"][...] = ref["mast"][mine, :] + ref["sum_recv"][0]
        if k == 2:
            ref["sum"][mine, :] = ref["sum_send"][...] + ref["sum_recv"][1]
        if k < 3:
            sum_copy(k).start()

    steps = {
        "dot": do_dot,
        "far": do_far,
        "near": do_near,
        "final": do_final,
        "update": do_update,
        "send": do_send,
        "pass": do_pass,
        "product": do_product,
        "sum": do_sum,
    }

    mast_copy.wait()
    for copy in row_copies:
        copy.start()
    ref["weight"][0, 0, 0] = jnp.transpose(ref["mast"][...]).astype(BF16)
    pl.semaphore_wait(barrier, len(to))

    row_order = (2, 1, 3, 0)
    loaded = set()
    for name, needs, _, _, _ in in_order(make_tasks()):
        if name[0] == "dot":
            if not loaded:
                grad_copy.wait()
                ref["grad_t"][...] = jnp.transpose(ref["grad"][...].astype(F32)).astype(BF16)
            y = SHARDS[name[1]]["y"]
            if y not in loaded:
                loaded.add(y)
                row_copies[row_order.index(y)].wait()
                if len(loaded) == 4:
                    for copy in state_copies:
                        copy.start()
        for token in needs:
            wait_for(token)
        with jax.named_scope(name[0]):
            steps[name[0]](*name[1:])

    end = jax.named_scope("left")
    end.__enter__()
    for p in range(len(REDUCE)):
        for sem in (ref[f"rs{p}"], ref[f"gs{p}"]):
            remote(ref[f"send{p}"], ref[f"recv{p}"], sem, sem, to["z"]).wait_send()
    for k in range(3):
        sum_copy(k).wait_send()
    end.__exit__(None, None, None)


def write_out(*refs):
    count = len(refs) // 2
    sem = refs[-1]
    copies = []
    for k in range(count):
        src, dst = refs[k], refs[count + k]
        cuts = 8 if k == 0 else 1
        rows = src.shape[0] // cuts
        for c in range(cuts):
            part = pl.ds(c * rows, rows)
            copies.append(pltpu.make_async_copy(src.at[part], dst.at[part], sem.at[len(copies)]))
    for copy in copies:
        copy.start()
    for copy in copies:
        copy.wait()


def exchange(*args):
    own = layout()
    shapes = [((TOK, 32 * SHARD), BF16)] + [((SHARD, COLS), F32)] * 5
    results = pl.pallas_call(
        functools.partial(kernel, tuple(own.names)),
        out_shape=[pltpu.VMEM(*shape) for shape in shapes],
        in_specs=[pl.BlockSpec(memory_space=pltpu.HBM)] * 7,
        out_specs=[pl.BlockSpec(memory_space=pltpu.VMEM)] * 6,
        scratch_shapes=own.shapes,
        compiler_params=pltpu.CompilerParams(collective_id=0, has_side_effects=True, vmem_limit_bytes=53 << 20),
        cost_estimate=pl.CostEstimate(flops=2 * 2 * TOK * COLS * 32 * SHARD, bytes_accessed=20 << 20, transcendentals=0),
    )(*args)
    return pl.pallas_call(
        write_out,
        out_shape=[jax.ShapeDtypeStruct(*shape) for shape in shapes],
        in_specs=[pl.BlockSpec(memory_space=pltpu.VMEM)] * 6,
        out_specs=[pl.BlockSpec(memory_space=pltpu.HBM)] * 6,
        scratch_shapes=[pltpu.SemaphoreType.DMA((13,))],
        compiler_params=pltpu.CompilerParams(vmem_limit_bytes=4 << 20),
    )(*[pltpu.with_memory_space_constraint(r, pltpu.VMEM) for r in results])


def on_device(layer_input, out_grad, master, first_moment, second_moment, anchor, outer_moment):
    input_grad, master_new, first_new, second_new, anchor_new, outer_new = exchange(
        layer_input, out_grad, master[0], first_moment[0], second_moment[0], anchor, outer_moment
    )
    return (input_grad, master_new[None], first_new[None], second_new[None], anchor_new, outer_new)


def solution(mesh):
    return jax.shard_map(
        on_device,
        mesh=mesh,
        in_specs=(
            P(("rep", "fsdp"), None),
            P(("rep", "fsdp"), None),
            P("rep", "fsdp", None),
            P("rep", "fsdp", None),
            P("rep", "fsdp", None),
            P("fsdp", None),
            P("fsdp", None),
        ),
        out_specs=(
            P(("rep", "fsdp"), None),
            P("rep", "fsdp", None),
            P("rep", "fsdp", None),
            P("rep", "fsdp", None),
            P("fsdp", None),
            P("fsdp", None),
        ),
        check_vma=False,
    )
```

```python
import functools

import jax
import jax.numpy as jnp
from jax import lax
from jax.experimental import pallas as pl
from jax.experimental.pallas import tpu as pltpu
from jax.sharding import PartitionSpec as P

MESH = pl.DeviceIdType.MESH
BF16 = jnp.bfloat16
F32 = jnp.float32

beta_one = 0.9
beta_two = 0.95
bias_one = 1.0 - 0.9**20
bias_two = 1.0 - 0.95**20

SHARD = 256
COLS = 512
TOK = 512
SIZE = {"y": 4, "x": 4, "z": 2}
SHARDS = tuple({"y": y, "x": x, "z": z} for y in range(4) for x in range(4) for z in range(2))

REDUCE = (
    (0, 176, 96, "yxz", (2, 2, 1)),
    (176, 176, 80, "xyz", (2, 2, 1)),
    (352, 80, 32, "zyx", (4, 2, 1)),
    (432, 80, 48, "zxy", (4, 2, 1)),
)
GATHER = (
    (0, 176, 80, "yxz", (2, 1, 1)),
    (176, 176, 96, "xyz", (2, 1, 1)),
    (352, 80, 48, "zyx", (4, 2, 1)),
    (432, 80, 32, "zxy", (4, 2, 1)),
)

RATE, MESSAGE, DELAY = 48448.7, 0.05, 2.271
DOT, PRODUCT, ADD, SEND = 0.40, 0.38, 0.0005, 0.02
AHEAD = 3.042
RANK = {
    "far": ((3.47, 14.97, 17.22), (-2.73, 34.93, 2.84)),
    "near": ((6.27, 21.7, 10.27), (31.86, 16.78, 25.62)),
    "send": ((12.08, 3.9, 9.83), (32.06, 7.23, 0.08)),
    "pass": ((25.72, 22.74, 16.64), (20.22, 7.85, 10.75)),
}


def count_of(dims):
    total = 1
    for d in dims:
        total *= SIZE[d]
    return total


def slot_of(dims, offsets):
    at = 0
    for d in dims:
        at = at * SIZE[d] + offsets[d]
    return at


def choices(dims):
    found = [{}]
    for d in dims:
        found = [{**o, d: k} for o in found for k in range(SIZE[d])]
    return found


def links_of(d):
    return ("z",) if d == "z" else ("+" + d, "-" + d)


def groups_of(parts, p, s):
    _, _, _, order, together = parts[p]
    inner = choices(order[s + 1 :])
    return [inner[k : k + together[s]] for k in range(0, len(inner), together[s])]


def block_of(p, s, buf, slot):
    order = REDUCE[p][3]
    sizes = [count_of(order[t + 1 :]) * (1 if order[t] == "z" else 3) for t in range(s)]
    return sum(sizes) + buf * count_of(order[s + 1 :]) + slot


def group_with(parts, p, s, o):
    _, _, _, order, together = parts[p]
    return slot_of(order[s + 1 :], o) // together[s]


def make_tasks():
    tasks = []

    def add(name, needs, time, sends, rank):
        if name[0] in RANK:
            rank = RANK[name[0]][name[1] // 2][name[2]]
        tasks.append((name, tuple(dict.fromkeys(needs)), time + SEND * len(sends), tuple(sends), rank))

    def term_needs(p, s, o):
        order = REDUCE[p][3]
        needs = [("dot", slot_of("yxz", o))]
        for t in range(s):
            needs.append(("reduce", p, t, group_with(REDUCE, p, t, o), 0 if order[t] == "z" else 1))
        return needs

    for o in SHARDS:
        far = (o["y"] == 2) + (o["x"] == 2)
        add(("dot", slot_of("yxz", o)), [], DOT, [], 22 - 2 * far - o["z"])
    for p, (_, n, low, order, together) in enumerate(REDUCE):
        for s in range(3):
            d, g = order[s], together[s]
            for at, group in enumerate(groups_of(REDUCE, p, s)):
                zero = {e: 0 for e in order[:s]}
                sizes = (n,) if d == "z" else (low, n - low)
                sends = [(link, g * size * 512, ("reduce", p, s, at, 0)) for link, size in zip(links_of(d), sizes)]
                needs = [t for o in group for t in term_needs(p, s, {**zero, **o, d: 1 if d == "z" else 2})]
                add(("far", p, s, at), needs, ADD * n * s * g, sends, 10)
                if d != "z":
                    needs = [t for o in group for k in (1, 3) for t in term_needs(p, s, {**zero, **o, d: k})] + [("reduce", p, s, at, 0)]
                    sends = [(link, g * n * 512, ("reduce", p, s, at, 1)) for link in links_of(d)]
                    add(("near", p, s, at), needs, ADD * n * (s + 1) * g * 2, sends, 10)
        add(("final", p), term_needs(p, 3, {"y": 0, "x": 0, "z": 0}), ADD * n * 4, [], 10)

    arrivals = {slot: [] for slot in range(32)}
    for p, (_, n, low, order, together) in enumerate(GATHER):
        have = {0: []}
        for s in (2, 1, 0):
            d, g = order[s], together[s]
            rank = 30 if s == 0 else 0
            zero = {e: 0 for e in order[: s + 1]}
            new = dict(have)
            for at, group in enumerate(groups_of(GATHER, p, s)):
                needs = [t for o in group for t in have[slot_of("yxz", {**zero, **o})]]
                token = [("gather", p, s, at, k) for k in range(2)]
                add(("send", p, s, at), needs, 0.0, [(link, g * n * 512, token[0]) for link in links_of(d)], rank)
                found = {1: [token[0]]}
                if d != "z":
                    sends = [("+" + d, g * low * 512, token[1]), ("-" + d, g * (n - low) * 512, token[1])]
                    add(("pass", p, s, at), [token[0]], 0.0, sends, rank)
                    found = {3: [token[0]], 1: [token[0]], 2: [token[1]]}
                for k, tokens in found.items():
                    for o in group:
                        new[slot_of("yxz", {**zero, **o, d: k})] = tokens
            have = new
        for slot, tokens in have.items():
            arrivals[slot] += tokens
    for slot in range(32):
        add(("product", slot), arrivals[slot] + [("dot", k) for k in range(32)], PRODUCT, [], 90)

    add(("sum", 0), [], 0.0, [("core", SHARD * COLS * 2, ("sum", "in", 0))], 1)
    add(("sum", 1), [("sum", "in", 0)], 0.1, [("z", SHARD * COLS * 2, ("sum", "in", 1))], 11)
    add(("sum", 2), [("sum", "in", 1)], 0.1, [("core", SHARD * COLS * 2, ("sum", "in", 2))], 12)
    add(("update",), [("sum", "in", 2)] + [("final", p) for p in range(len(REDUCE))], 1.0, [], 80)
    return tasks


def in_order(tasks):
    now, done, free, order = 0.0, {}, {}, []
    left = sorted(tasks, key=lambda task: task[4])
    while left:
        ready, soonest = None, None
        for task in left:
            if task[0][0] in ("send", "pass") and task[0][2] == 0 and any(free.get(link, 0.0) > now + AHEAD for link, _, _ in task[3]):
                at = max(free.get(link, 0.0) - AHEAD for link, _, _ in task[3])
                soonest = at if soonest is None else min(soonest, at)
            elif all(token in done for token in task[1]):
                at = max([done[token] for token in task[1]], default=0.0)
                if at <= now:
                    ready = task
                    break
                soonest = at if soonest is None else min(soonest, at)
        if ready is None:
            now = max(soonest, now + 0.001)
            continue
        left.remove(ready)
        order.append(ready)
        now += ready[2]
        done[ready[0]] = now
        for link, size, token in ready[3]:
            rate = 12 * RATE if link == "core" else RATE
            free[link] = max(free.get(link, 0.0), now) + size / rate + MESSAGE
            done[token] = max(done.get(token, 0.0), free[link] + DELAY)
    return order


class Layout:
    def __init__(self):
        self.names, self.shapes = [], []

    def add(self, name, shape):
        self.names.append(name)
        self.shapes.append(shape)


def layout():
    own = Layout()
    own.add("grad", pltpu.VMEM((TOK, COLS), BF16))
    own.add("grad_t", pltpu.VMEM((COLS, TOK), BF16))
    own.add("mast", pltpu.VMEM((SHARD, COLS), F32))
    own.add("weight", pltpu.VMEM((4, 4, 2, COLS, SHARD), BF16))
    own.add("term", pltpu.VMEM((32, COLS, SHARD), F32))
    own.add("sum_send", pltpu.VMEM((SHARD // 2, COLS), F32))
    own.add("sum_recv", pltpu.VMEM((2, SHARD // 2, COLS), F32))
    own.add("sum", pltpu.VMEM((SHARD, COLS), F32))
    own.add("sum_ss", pltpu.SemaphoreType.DMA((3,)))
    own.add("sum_rs", pltpu.SemaphoreType.DMA((3,)))
    own.add("grad_sum", pltpu.VMEM((COLS, SHARD), F32))
    own.add("state", pltpu.VMEM((4, SHARD, COLS), F32))
    own.add("in_sem", pltpu.SemaphoreType.DMA((7,)))
    for p, (_, n, _, _, _) in enumerate(REDUCE):
        own.add(f"send{p}", pltpu.VMEM((31, n, SHARD), BF16))
        own.add(f"recv{p}", pltpu.VMEM((31, n, SHARD), BF16))
    for parts, one, two in ((REDUCE, "rs", "rr"), (GATHER, "gs", "gr")):
        for p in range(len(parts)):
            own.add(f"{one}{p}", pltpu.SemaphoreType.DMA)
            for s in range(3):
                own.add(f"{two}{p}{s}", pltpu.SemaphoreType.DMA((len(links_of(parts[p][3][s])), len(groups_of(parts, p, s)))))
    return own


def kernel(names, rows_hbm, grad_hbm, mast_hbm, first_hbm, second_hbm, anchor_hbm, outer_hbm, out_ref, *refs):
    new_master, new_first, new_second, new_anchor, new_outer = refs[:5]
    refs = refs[5:]
    ref = dict(zip(names, refs))
    rep, fsdp = lax.axis_index("rep"), lax.axis_index("fsdp")
    me = {"y": fsdp // 8, "x": fsdp // 2 % 4, "z": fsdp % 2}
    core = rep % 2
    place = {d: [(me[d] + k) % SIZE[d] for k in range(SIZE[d])] for d in "yxz"}

    def device(y, x, z):
        return (rep, (y * 4 + x) * 2 + z)

    to = {
        "+y": device(place["y"][1], me["x"], me["z"]),
        "-y": device(place["y"][3], me["x"], me["z"]),
        "+x": device(me["y"], place["x"][1], me["z"]),
        "-x": device(me["y"], place["x"][3], me["z"]),
        "z": device(me["y"], me["x"], place["z"][1]),
        "core": (rep + 1 - 2 * core, fsdp),
        "far": ((rep + 2) % 4, fsdp),
    }

    barrier = pltpu.get_barrier_semaphore()
    for target in to.values():
        pl.semaphore_signal(barrier, inc=1, device_id=target, device_id_type=MESH)

    mast_copy = pltpu.make_async_copy(mast_hbm, ref["mast"], ref["in_sem"].at[4])
    grad_copy = pltpu.make_async_copy(grad_hbm, ref["grad"], ref["in_sem"].at[5])
    row_copies = []
    for k in range(4):
        columns = pl.ds(pl.multiple_of(place["y"][(2, 1, 3, 0)[k]] * (8 * SHARD), 8 * SHARD), 8 * SHARD)
        row_copies.append(pltpu.make_async_copy(rows_hbm.at[:, columns], out_ref.at[:, columns], ref["in_sem"].at[k]))
    state_copies = []
    for k, hbm in enumerate((first_hbm, second_hbm, anchor_hbm, outer_hbm)):
        state_copies.append(pltpu.make_async_copy(hbm, ref["state"].at[k], ref["in_sem"].at[6]))
    mast_copy.start()
    grad_copy.start()

    def columns_of(o):
        y, x, z = [place[d][o[d]] for d in "yxz"]
        return pl.ds(pl.multiple_of(((y * 4 + x) * 2 + z) * SHARD, SHARD), SHARD)

    def remote(src, dst, send_sem, recv_sem, target):
        return pltpu.make_async_remote_copy(
            src_ref=src, dst_ref=dst, send_sem=send_sem, recv_sem=recv_sem, device_id=target, device_id_type=MESH
        )

    half = SHARD // 2
    mine = pl.ds(pl.multiple_of(core * half, half), half)
    other = pl.ds(pl.multiple_of((1 - core) * half, half), half)

    def sum_copy(k):
        src, dst, target = (
            (ref["mast"].at[other], ref["sum_recv"].at[0], to["core"]),
            (ref["sum_send"], ref["sum_recv"].at[1], to["far"]),
            (ref["sum"].at[mine], ref["sum"].at[mine], to["core"]),
        )[k]
        return remote(src, dst, ref["sum_ss"].at[k], ref["sum_rs"].at[k], target)

    def weight_at(d, at, group, first, count):
        index = []
        for e in "yxz":
            if e == d:
                index.append(at)
            elif e in group[0] and group[0][e] != group[-1][e]:
                index.append(pl.ds(group[0][e], group[-1][e] - group[0][e] + 1))
            else:
                index.append(group[0].get(e, 0))
        return ref["weight"].at[(*index, pl.ds(first, count))]

    def gather_copy(p, s, at, kind):
        first, n, low, order, _ = GATHER[p]
        d = order[s]
        if d == "z":
            src, dst, a, c, link = 0, 1, first, n, "z"
        else:
            src, dst, a, c, link = (
                (0, 3, first, n, "+" + d),
                (0, 1, first, n, "-" + d),
                (3, 2, first, low, "+" + d),
                (1, 2, first + low, n - low, "-" + d),
            )[kind]
        group = groups_of(GATHER, p, s)[at]
        return remote(
            weight_at(d, src, group, a, c),
            weight_at(d, dst, group, a, c),
            ref[f"gs{p}"],
            ref[f"gr{p}{s}"].at[kind // 2, at],
            to[link],
        )

    def reduce_copy(p, s, at, kind):
        _, n, low, order, together = REDUCE[p]
        d = order[s]
        if d == "z":
            buf, a, c, link = 0, 0, n, "z"
        else:
            buf, a, c, link = (
                (0, 0, low, "+" + d),
                (0, low, n - low, "-" + d),
                (1, 0, n, "+" + d),
                (2, 0, n, "-" + d),
            )[kind]
        slots = pl.ds(block_of(p, s, buf, at * together[s]), together[s])
        return remote(
            ref[f"send{p}"].at[slots, pl.ds(a, c)],
            ref[f"recv{p}"].at[slots, pl.ds(a, c)],
            ref[f"rs{p}"],
            ref[f"rr{p}{s}"].at[kind // 2, at],
            to[link],
        )

    def gather_wait(p, s, at, phase):
        first, n, _, order, _ = GATHER[p]
        d, group = order[s], groups_of(GATHER, p, s)[at]
        where = 1 if d == "z" else 2 if phase else pl.ds(0, 2)
        block, sem = weight_at(d, where, group, first, n), ref[f"gr{p}{s}"].at[phase, at]
        remote(block, block, sem, sem, to["z"]).wait_recv()

    def reduce_wait(p, s, at, phase):
        _, n, _, order, together = REDUCE[p]
        g, sem = together[s], ref[f"rr{p}{s}"].at[phase, at]
        count = 2 * g if phase else g
        block = ref[f"recv{p}"].at[pl.ds(block_of(p, s, phase, at * g), count)]
        remote(block, block, sem, sem, to["z"]).wait_recv()

    waited = set()

    def wait_for(token):
        if token in waited or (token[0] not in ("reduce", "gather") and "in" not in token):
            return
        waited.add(token)
        if token[0] == "sum":
            sum_copy(token[2]).wait_recv()
        else:
            (reduce_wait if token[0] == "reduce" else gather_wait)(*token[1:])

    def term(p, s, o):
        first, n, _, order, _ = REDUCE[p]
        value = ref["term"][slot_of("yxz", o), first : first + n, :]
        for t in range(s):
            slot = slot_of(order[t + 1 :], o)
            for buf in (0,) if order[t] == "z" else (1, 2):
                value = value + ref[f"recv{p}"][block_of(p, t, buf, slot)].astype(F32)
        return value

    def do_dot(slot):
        o = SHARDS[slot]
        value = jnp.dot(ref["grad_t"][...], out_ref[:, columns_of(o)], preferred_element_type=F32)
        for p, (first, n, _, order, _) in enumerate(REDUCE):
            d = order[0]
            piece = value[first : first + n, :]
            if o[d] == (1 if d == "z" else 2):
                ref[f"send{p}"][slot_of(order[1:], o)] = piece.astype(BF16)
            else:
                ref["term"][slot, first : first + n, :] = piece

    def do_far(p, s, at):
        order = REDUCE[p][3]
        d = order[s]
        for inner in groups_of(REDUCE, p, s)[at] if s else ():
            o = {**{e: 0 for e in order[:s]}, **inner, d: 1 if d == "z" else 2}
            ref[f"send{p}"][block_of(p, s, 0, slot_of(order[s + 1 :], inner))] = term(p, s, o).astype(BF16)
        for kind in range(len(links_of(d))):
            reduce_copy(p, s, at, kind).start()

    def do_near(p, s, at):
        _, n, low, order, _ = REDUCE[p]
        send, recv = ref[f"send{p}"], ref[f"recv{p}"]
        for kind in (0, 1):
            for inner in groups_of(REDUCE, p, s)[at]:
                value = term(p, s, {**{e: 0 for e in order[:s]}, **inner, order[s]: 1 + 2 * kind})
                slot = slot_of(order[s + 1 :], inner)
                came, goes = block_of(p, s, 0, slot), block_of(p, s, kind + 1, slot)
                for which, (a, b) in enumerate(((0, low), (low, n))):
                    piece = value[a:b]
                    if which == kind:
                        piece = piece + recv[came, a:b].astype(F32)
                    send[goes, a:b] = piece.astype(BF16)
            reduce_copy(p, s, at, kind + 2).start()

    def do_final(p):
        first, n = REDUCE[p][:2]
        ref["grad_sum"][first : first + n, :] = term(p, 3, {"y": 0, "x": 0, "z": 0})

    def do_update():
        pltpu.make_async_copy(ref["state"], ref["state"], ref["in_sem"].at[6]).wait()

        gradient_t = ref["grad_sum"]
        for k in range(2):
            rows = slice(k * 128, k * 128 + 128)
            gradient = jnp.transpose(gradient_t[:, rows])
            master = ref["mast"][rows, :]
            first_new = beta_one * ref["state"][0, rows, :] + (1.0 - beta_one) * gradient
            second_new = beta_two * ref["state"][1, rows, :] + (1.0 - beta_two) * gradient * gradient
            update = first_new / bias_one / (jnp.sqrt(second_new / bias_two) + 1e-08)
            inner = master - 0.002 * (update + 0.1 * master)
            anchor = ref["state"][2, rows, :]
            delta = anchor - ref["sum"][rows, :] / 4.0
            outer_new = 0.9 * ref["state"][3, rows, :] + delta
            anchor_new = anchor - 0.7 * (0.9 * outer_new + delta)
            new_first[rows, :] = first_new
            new_second[rows, :] = second_new
            new_outer[rows, :] = outer_new
            new_anchor[rows, :] = anchor_new
            new_master[rows, :] = 0.5 * inner + 0.5 * anchor_new

    def do_send(p, s, at):
        for kind in range(len(links_of(GATHER[p][3][s]))):
            gather_copy(p, s, at, kind).start()

    def do_pass(p, s, at):
        gather_copy(p, s, at, 2).start()
        gather_copy(p, s, at, 3).start()

    def do_product(slot):
        value = jnp.dot(ref["grad"][...], ref["weight"][tuple(SHARDS[slot].values())], preferred_element_type=F32)
        out_ref[:, columns_of(SHARDS[slot])] = value.astype(BF16)

    def do_sum(k):
        if k == 1:
            ref["sum_send"][...] = ref["mast"][mine, :] + ref["sum_recv"][0]
        if k == 2:
            ref["sum"][mine, :] = ref["sum_send"][...] + ref["sum_recv"][1]
        if k < 3:
            sum_copy(k).start()

    steps = {
        "dot": do_dot,
        "far": do_far,
        "near": do_near,
        "final": do_final,
        "update": do_update,
        "send": do_send,
        "pass": do_pass,
        "product": do_product,
        "sum": do_sum,
    }

    mast_copy.wait()
    for copy in row_copies:
        copy.start()
    ref["weight"][0, 0, 0] = jnp.transpose(ref["mast"][...]).astype(BF16)
    pl.semaphore_wait(barrier, len(to))

    row_order = (2, 1, 3, 0)
    loaded = set()
    for name, needs, _, _, _ in in_order(make_tasks()):
        if name[0] == "dot":
            if not loaded:
                grad_copy.wait()
                ref["grad_t"][...] = jnp.transpose(ref["grad"][...].astype(F32)).astype(BF16)
            y = SHARDS[name[1]]["y"]
            if y not in loaded:
                loaded.add(y)
                row_copies[row_order.index(y)].wait()
                if len(loaded) == 4:
                    for copy in state_copies:
                        copy.start()
        for token in needs:
            wait_for(token)
        with jax.named_scope(name[0]):
            steps[name[0]](*name[1:])

    for p in range(len(REDUCE)):
        for sem in (ref[f"rs{p}"], ref[f"gs{p}"]):
            remote(ref[f"send{p}"], ref[f"recv{p}"], sem, sem, to["z"]).wait_send()
    for k in range(3):
        sum_copy(k).wait_send()


def write_out(*refs):
    count = len(refs) // 2
    sem = refs[-1]
    copies = []
    for k in range(count):
        src, dst = refs[k], refs[count + k]
        cuts = 8 if k == 0 else 1
        rows = src.shape[0] // cuts
        for c in range(cuts):
            part = pl.ds(c * rows, rows)
            copies.append(pltpu.make_async_copy(src.at[part], dst.at[part], sem.at[len(copies)]))
    for copy in copies:
        copy.start()
    for copy in copies:
        copy.wait()


def exchange(*args):
    own = layout()
    shapes = [((TOK, 32 * SHARD), BF16)] + [((SHARD, COLS), F32)] * 5
    results = pl.pallas_call(
        functools.partial(kernel, tuple(own.names)),
        out_shape=[pltpu.VMEM(*shape) for shape in shapes],
        in_specs=[pl.BlockSpec(memory_space=pltpu.HBM)] * 7,
        out_specs=[pl.BlockSpec(memory_space=pltpu.VMEM)] * 6,
        scratch_shapes=own.shapes,
        compiler_params=pltpu.CompilerParams(collective_id=0, has_side_effects=True, vmem_limit_bytes=53 << 20),
        cost_estimate=pl.CostEstimate(flops=2 * 2 * TOK * COLS * 32 * SHARD, bytes_accessed=20 << 20, transcendentals=0),
    )(*args)
    return pl.pallas_call(
        write_out,
        out_shape=[jax.ShapeDtypeStruct(*shape) for shape in shapes],
        in_specs=[pl.BlockSpec(memory_space=pltpu.VMEM)] * 6,
        out_specs=[pl.BlockSpec(memory_space=pltpu.HBM)] * 6,
        scratch_shapes=[pltpu.SemaphoreType.DMA((13,))],
        compiler_params=pltpu.CompilerParams(vmem_limit_bytes=4 << 20),
    )(*[pltpu.with_memory_space_constraint(r, pltpu.VMEM) for r in results])


def on_device(layer_input, out_grad, master, first_moment, second_moment, anchor, outer_moment):
    input_grad, master_new, first_new, second_new, anchor_new, outer_new = exchange(
        layer_input, out_grad, master[0], first_moment[0], second_moment[0], anchor, outer_moment
    )
    return (input_grad, master_new[None], first_new[None], second_new[None], anchor_new, outer_new)


def solution(mesh):
    return jax.shard_map(
        on_device,
        mesh=mesh,
        in_specs=(
            P(("rep", "fsdp"), None),
            P(("rep", "fsdp"), None),
            P("rep", "fsdp", None),
            P("rep", "fsdp", None),
            P("rep", "fsdp", None),
            P("fsdp", None),
            P("fsdp", None),
        ),
        out_specs=(
            P(("rep", "fsdp"), None),
            P("rep", "fsdp", None),
            P("rep", "fsdp", None),
            P("rep", "fsdp", None),
            P("fsdp", None),
            P("fsdp", None),
        ),
        check_vma=False,
    )
```

```python
import functools

import jax
import jax.numpy as jnp
from jax import lax
from jax.experimental import pallas as pl
from jax.experimental.pallas import tpu as pltpu
from jax.sharding import PartitionSpec as P

MESH = pl.DeviceIdType.MESH
BF16 = jnp.bfloat16
F32 = jnp.float32

beta_one = 0.9
beta_two = 0.95
bias_one = 1.0 - 0.9**20
bias_two = 1.0 - 0.95**20

SHARD = 256
COLS = 512
TOK = 512
SIZE = {"y": 4, "x": 4, "z": 2}
SHARDS = tuple({"y": y, "x": x, "z": z} for y in range(4) for x in range(4) for z in range(2))

REDUCE = (
    (0, 176, 96, "yxz", (2, 2, 1)),
    (176, 176, 80, "xyz", (2, 2, 1)),
    (352, 80, 32, "zyx", (4, 2, 1)),
    (432, 80, 48, "zxy", (4, 2, 1)),
)
GATHER = (
    (0, 176, 80, "yxz", (2, 1, 1)),
    (176, 176, 96, "xyz", (2, 1, 1)),
    (352, 80, 48, "zyx", (4, 2, 1)),
    (432, 80, 32, "zxy", (4, 2, 1)),
)

RATE, MESSAGE, DELAY = 48448.7, 0.05, 2.271
DOT, PRODUCT, ADD, SEND = 0.40, 0.38, 0.0005, 0.02
AHEAD = 3.042
RANK = {
    "far": ((3.47, 14.97, 17.22), (-2.73, 34.93, 2.84)),
    "near": ((6.27, 21.7, 10.27), (31.86, 16.78, 25.62)),
    "send": ((12.08, 3.9, 9.83), (32.06, 7.23, 0.08)),
    "pass": ((25.72, 22.74, 16.64), (20.22, 7.85, 10.75)),
}


def count_of(dims):
    total = 1
    for d in dims:
        total *= SIZE[d]
    return total


def slot_of(dims, offsets):
    at = 0
    for d in dims:
        at = at * SIZE[d] + offsets[d]
    return at


def choices(dims):
    found = [{}]
    for d in dims:
        found = [{**o, d: k} for o in found for k in range(SIZE[d])]
    return found


def links_of(d):
    return ("z",) if d == "z" else ("+" + d, "-" + d)


def groups_of(parts, p, s):
    _, _, _, order, together = parts[p]
    inner = choices(order[s + 1 :])
    return [inner[k : k + together[s]] for k in range(0, len(inner), together[s])]


def block_of(p, s, buf, slot):
    order = REDUCE[p][3]
    sizes = [count_of(order[t + 1 :]) * (1 if order[t] == "z" else 3) for t in range(s)]
    return sum(sizes) + buf * count_of(order[s + 1 :]) + slot


def group_with(parts, p, s, o):
    _, _, _, order, together = parts[p]
    return slot_of(order[s + 1 :], o) // together[s]


def make_tasks():
    tasks = []

    def add(name, needs, time, sends, rank):
        if name[0] in RANK:
            rank = RANK[name[0]][name[1] // 2][name[2]]
        tasks.append((name, tuple(dict.fromkeys(needs)), time + SEND * len(sends), tuple(sends), rank))

    def term_needs(p, s, o):
        order = REDUCE[p][3]
        needs = [("dot", slot_of("yxz", o))]
        for t in range(s):
            needs.append(("reduce", p, t, group_with(REDUCE, p, t, o), 0 if order[t] == "z" else 1))
        return needs

    for o in SHARDS:
        far = (o["y"] == 2) + (o["x"] == 2)
        add(("dot", slot_of("yxz", o)), [], DOT, [], 22 - 2 * far - o["z"])
    for p, (_, n, low, order, together) in enumerate(REDUCE):
        for s in range(3):
            d, g = order[s], together[s]
            for at, group in enumerate(groups_of(REDUCE, p, s)):
                zero = {e: 0 for e in order[:s]}
                sizes = (n,) if d == "z" else (low, n - low)
                sends = [(link, g * size * 512, ("reduce", p, s, at, 0)) for link, size in zip(links_of(d), sizes)]
                needs = [t for o in group for t in term_needs(p, s, {**zero, **o, d: 1 if d == "z" else 2})]
                add(("far", p, s, at), needs, ADD * n * s * g, sends, 10)
                if d != "z":
                    needs = [t for o in group for k in (1, 3) for t in term_needs(p, s, {**zero, **o, d: k})] + [("reduce", p, s, at, 0)]
                    sends = [(link, g * n * 512, ("reduce", p, s, at, 1)) for link in links_of(d)]
                    add(("near", p, s, at), needs, ADD * n * (s + 1) * g * 2, sends, 10)
        add(("final", p), term_needs(p, 3, {"y": 0, "x": 0, "z": 0}), ADD * n * 4, [], 10)

    arrivals = {slot: [] for slot in range(32)}
    for p, (_, n, low, order, together) in enumerate(GATHER):
        have = {0: []}
        for s in (2, 1, 0):
            d, g = order[s], together[s]
            rank = 30 if s == 0 else 0
            zero = {e: 0 for e in order[: s + 1]}
            new = dict(have)
            for at, group in enumerate(groups_of(GATHER, p, s)):
                needs = [t for o in group for t in have[slot_of("yxz", {**zero, **o})]]
                token = [("gather", p, s, at, k) for k in range(2)]
                add(("send", p, s, at), needs, 0.0, [(link, g * n * 512, token[0]) for link in links_of(d)], rank)
                found = {1: [token[0]]}
                if d != "z":
                    sends = [("+" + d, g * low * 512, token[1]), ("-" + d, g * (n - low) * 512, token[1])]
                    add(("pass", p, s, at), [token[0]], 0.0, sends, rank)
                    found = {3: [token[0]], 1: [token[0]], 2: [token[1]]}
                for k, tokens in found.items():
                    for o in group:
                        new[slot_of("yxz", {**zero, **o, d: k})] = tokens
            have = new
        for slot, tokens in have.items():
            arrivals[slot] += tokens
    for slot in range(32):
        add(("product", slot), arrivals[slot] + [("dot", k) for k in range(32)], PRODUCT, [], 90)

    add(("sum", 0), [], 0.0, [("core", SHARD * COLS * 2, ("sum", "in", 0))], 1)
    add(("sum", 1), [("sum", "in", 0)], 0.1, [("z", SHARD * COLS * 2, ("sum", "in", 1))], 11)
    add(("sum", 2), [("sum", "in", 1)], 0.1, [("core", SHARD * COLS * 2, ("sum", "in", 2))], 12)
    add(("update",), [("sum", "in", 2)] + [("final", p) for p in range(len(REDUCE))], 1.0, [], 80)
    return tasks


def in_order(tasks):
    now, done, free, order = 0.0, {}, {}, []
    left = sorted(tasks, key=lambda task: task[4])
    while left:
        ready, soonest = None, None
        for task in left:
            if task[0][0] in ("send", "pass") and task[0][2] == 0 and any(free.get(link, 0.0) > now + AHEAD for link, _, _ in task[3]):
                at = max(free.get(link, 0.0) - AHEAD for link, _, _ in task[3])
                soonest = at if soonest is None else min(soonest, at)
            elif all(token in done for token in task[1]):
                at = max([done[token] for token in task[1]], default=0.0)
                if at <= now:
                    ready = task
                    break
                soonest = at if soonest is None else min(soonest, at)
        if ready is None:
            now = max(soonest, now + 0.001)
            continue
        left.remove(ready)
        order.append(ready)
        now += ready[2]
        done[ready[0]] = now
        for link, size, token in ready[3]:
            rate = 12 * RATE if link == "core" else RATE
            free[link] = max(free.get(link, 0.0), now) + size / rate + MESSAGE
            done[token] = max(done.get(token, 0.0), free[link] + DELAY)
    return order


class Layout:
    def __init__(self):
        self.names, self.shapes = [], []

    def add(self, name, shape):
        self.names.append(name)
        self.shapes.append(shape)


def layout():
    own = Layout()
    own.add("grad", pltpu.VMEM((TOK, COLS), BF16))
    own.add("grad_t", pltpu.VMEM((COLS, TOK), BF16))
    own.add("mast", pltpu.VMEM((SHARD, COLS), F32))
    own.add("weight", pltpu.VMEM((4, 4, 2, COLS, SHARD), BF16))
    own.add("term", pltpu.VMEM((32, COLS, SHARD), F32))
    own.add("sum_send", pltpu.VMEM((SHARD // 2, COLS), F32))
    own.add("sum_recv", pltpu.VMEM((2, SHARD // 2, COLS), F32))
    own.add("sum", pltpu.VMEM((SHARD, COLS), F32))
    own.add("sum_ss", pltpu.SemaphoreType.DMA((3,)))
    own.add("sum_rs", pltpu.SemaphoreType.DMA((3,)))
    own.add("grad_sum", pltpu.VMEM((COLS, SHARD), F32))
    own.add("state", pltpu.VMEM((4, SHARD, COLS), F32))
    own.add("in_sem", pltpu.SemaphoreType.DMA((7,)))
    for p, (_, n, _, _, _) in enumerate(REDUCE):
        own.add(f"send{p}", pltpu.VMEM((31, n, SHARD), BF16))
        own.add(f"recv{p}", pltpu.VMEM((31, n, SHARD), BF16))
    for parts, one, two in ((REDUCE, "rs", "rr"), (GATHER, "gs", "gr")):
        for p in range(len(parts)):
            own.add(f"{one}{p}", pltpu.SemaphoreType.DMA)
            for s in range(3):
                own.add(f"{two}{p}{s}", pltpu.SemaphoreType.DMA((len(links_of(parts[p][3][s])), len(groups_of(parts, p, s)))))
    return own


def kernel(names, rows_hbm, grad_hbm, mast_hbm, first_hbm, second_hbm, anchor_hbm, outer_hbm, out_ref, *refs):
    new_master, new_first, new_second, new_anchor, new_outer = refs[:5]
    refs = refs[5:]
    ref = dict(zip(names, refs))
    rep, fsdp = lax.axis_index("rep"), lax.axis_index("fsdp")
    me = {"y": fsdp // 8, "x": fsdp // 2 % 4, "z": fsdp % 2}
    core = rep % 2
    place = {d: [(me[d] + k) % SIZE[d] for k in range(SIZE[d])] for d in "yxz"}

    def device(y, x, z):
        return (rep, (y * 4 + x) * 2 + z)

    to = {
        "+y": device(place["y"][1], me["x"], me["z"]),
        "-y": device(place["y"][3], me["x"], me["z"]),
        "+x": device(me["y"], place["x"][1], me["z"]),
        "-x": device(me["y"], place["x"][3], me["z"]),
        "z": device(me["y"], me["x"], place["z"][1]),
        "core": (rep + 1 - 2 * core, fsdp),
        "far": ((rep + 2) % 4, fsdp),
    }

    barrier = pltpu.get_barrier_semaphore()
    for target in to.values():
        pl.semaphore_signal(barrier, inc=1, device_id=target, device_id_type=MESH)

    mast_copy = pltpu.make_async_copy(mast_hbm, ref["mast"], ref["in_sem"].at[4])
    grad_copy = pltpu.make_async_copy(grad_hbm, ref["grad"], ref["in_sem"].at[5])
    row_copies = []
    for k in range(4):
        columns = pl.ds(pl.multiple_of(place["y"][(2, 1, 3, 0)[k]] * (8 * SHARD), 8 * SHARD), 8 * SHARD)
        row_copies.append(pltpu.make_async_copy(rows_hbm.at[:, columns], out_ref.at[:, columns], ref["in_sem"].at[k]))
    state_copies = []
    for k, hbm in enumerate((first_hbm, second_hbm, anchor_hbm, outer_hbm)):
        state_copies.append(pltpu.make_async_copy(hbm, ref["state"].at[k], ref["in_sem"].at[6]))
    mast_copy.start()
    grad_copy.start()

    def columns_of(o):
        y, x, z = [place[d][o[d]] for d in "yxz"]
        return pl.ds(pl.multiple_of(((y * 4 + x) * 2 + z) * SHARD, SHARD), SHARD)

    def remote(src, dst, send_sem, recv_sem, target):
        return pltpu.make_async_remote_copy(
            src_ref=src, dst_ref=dst, send_sem=send_sem, recv_sem=recv_sem, device_id=target, device_id_type=MESH
        )

    half = SHARD // 2
    mine = pl.ds(pl.multiple_of(core * half, half), half)
    other = pl.ds(pl.multiple_of((1 - core) * half, half), half)

    def sum_copy(k):
        src, dst, target = (
            (ref["mast"].at[other], ref["sum_recv"].at[0], to["core"]),
            (ref["sum_send"], ref["sum_recv"].at[1], to["far"]),
            (ref["sum"].at[mine], ref["sum"].at[mine], to["core"]),
        )[k]
        return remote(src, dst, ref["sum_ss"].at[k], ref["sum_rs"].at[k], target)

    def weight_at(d, at, group, first, count):
        index = []
        for e in "yxz":
            if e == d:
                index.append(at)
            elif e in group[0] and group[0][e] != group[-1][e]:
                index.append(pl.ds(group[0][e], group[-1][e] - group[0][e] + 1))
            else:
                index.append(group[0].get(e, 0))
        return ref["weight"].at[(*index, pl.ds(first, count))]

    def gather_copy(p, s, at, kind):
        first, n, low, order, _ = GATHER[p]
        d = order[s]
        if d == "z":
            src, dst, a, c, link = 0, 1, first, n, "z"
        else:
            src, dst, a, c, link = (
                (0, 3, first, n, "+" + d),
                (0, 1, first, n, "-" + d),
                (3, 2, first, low, "+" + d),
                (1, 2, first + low, n - low, "-" + d),
            )[kind]
        group = groups_of(GATHER, p, s)[at]
        return remote(
            weight_at(d, src, group, a, c),
            weight_at(d, dst, group, a, c),
            ref[f"gs{p}"],
            ref[f"gr{p}{s}"].at[kind // 2, at],
            to[link],
        )

    def reduce_copy(p, s, at, kind):
        _, n, low, order, together = REDUCE[p]
        d = order[s]
        if d == "z":
            buf, a, c, link = 0, 0, n, "z"
        else:
            buf, a, c, link = (
                (0, 0, low, "+" + d),
                (0, low, n - low, "-" + d),
                (1, 0, n, "+" + d),
                (2, 0, n, "-" + d),
            )[kind]
        slots = pl.ds(block_of(p, s, buf, at * together[s]), together[s])
        return remote(
            ref[f"send{p}"].at[slots, pl.ds(a, c)],
            ref[f"recv{p}"].at[slots, pl.ds(a, c)],
            ref[f"rs{p}"],
            ref[f"rr{p}{s}"].at[kind // 2, at],
            to[link],
        )

    def gather_wait(p, s, at, phase):
        first, n, _, order, _ = GATHER[p]
        d, group = order[s], groups_of(GATHER, p, s)[at]
        where = 1 if d == "z" else 2 if phase else pl.ds(0, 2)
        block, sem = weight_at(d, where, group, first, n), ref[f"gr{p}{s}"].at[phase, at]
        remote(block, block, sem, sem, to["z"]).wait_recv()

    def reduce_wait(p, s, at, phase):
        _, n, _, order, together = REDUCE[p]
        g, sem = together[s], ref[f"rr{p}{s}"].at[phase, at]
        count = 2 * g if phase else g
        block = ref[f"recv{p}"].at[pl.ds(block_of(p, s, phase, at * g), count)]
        remote(block, block, sem, sem, to["z"]).wait_recv()

    waited = set()

    def wait_for(token):
        if token in waited or (token[0] not in ("reduce", "gather") and "in" not in token):
            return
        waited.add(token)
        if token[0] == "sum":
            sum_copy(token[2]).wait_recv()
        else:
            (reduce_wait if token[0] == "reduce" else gather_wait)(*token[1:])

    def term(p, s, o):
        first, n, _, order, _ = REDUCE[p]
        value = ref["term"][slot_of("yxz", o), first : first + n, :]
        for t in range(s):
            slot = slot_of(order[t + 1 :], o)
            for buf in (0,) if order[t] == "z" else (1, 2):
                value = value + ref[f"recv{p}"][block_of(p, t, buf, slot)].astype(F32)
        return value

    def do_dot(slot):
        o = SHARDS[slot]
        value = jnp.dot(ref["grad_t"][...], out_ref[:, columns_of(o)], preferred_element_type=F32)
        for p, (first, n, _, order, _) in enumerate(REDUCE):
            d = order[0]
            piece = value[first : first + n, :]
            if o[d] == (1 if d == "z" else 2):
                ref[f"send{p}"][slot_of(order[1:], o)] = piece.astype(BF16)
            else:
                ref["term"][slot, first : first + n, :] = piece

    def do_far(p, s, at):
        order = REDUCE[p][3]
        d = order[s]
        for inner in groups_of(REDUCE, p, s)[at] if s else ():
            o = {**{e: 0 for e in order[:s]}, **inner, d: 1 if d == "z" else 2}
            ref[f"send{p}"][block_of(p, s, 0, slot_of(order[s + 1 :], inner))] = term(p, s, o).astype(BF16)
        for kind in range(len(links_of(d))):
            reduce_copy(p, s, at, kind).start()

    def do_near(p, s, at):
        _, n, low, order, _ = REDUCE[p]
        send, recv = ref[f"send{p}"], ref[f"recv{p}"]
        for kind in (0, 1):
            for inner in groups_of(REDUCE, p, s)[at]:
                value = term(p, s, {**{e: 0 for e in order[:s]}, **inner, order[s]: 1 + 2 * kind})
                slot = slot_of(order[s + 1 :], inner)
                came, goes = block_of(p, s, 0, slot), block_of(p, s, kind + 1, slot)
                for which, (a, b) in enumerate(((0, low), (low, n))):
                    piece = value[a:b]
                    if which == kind:
                        piece = piece + recv[came, a:b].astype(F32)
                    send[goes, a:b] = piece.astype(BF16)
            reduce_copy(p, s, at, kind + 2).start()

    def do_final(p):
        first, n = REDUCE[p][:2]
        ref["grad_sum"][first : first + n, :] = term(p, 3, {"y": 0, "x": 0, "z": 0})

    def do_update():
        pltpu.make_async_copy(ref["state"], ref["state"], ref["in_sem"].at[6]).wait()

        gradient_t = ref["grad_sum"]
        for k in range(2):
            rows = slice(k * 128, k * 128 + 128)
            gradient = jnp.transpose(gradient_t[:, rows])
            master = ref["mast"][rows, :]
            first_new = beta_one * ref["state"][0, rows, :] + (1.0 - beta_one) * gradient
            second_new = beta_two * ref["state"][1, rows, :] + (1.0 - beta_two) * gradient * gradient
            update = first_new / bias_one / (jnp.sqrt(second_new / bias_two) + 1e-08)
            inner = master - 0.002 * (update + 0.1 * master)
            anchor = ref["state"][2, rows, :]
            delta = anchor - ref["sum"][rows, :] / 4.0
            outer_new = 0.9 * ref["state"][3, rows, :] + delta
            anchor_new = anchor - 0.7 * (0.9 * outer_new + delta)
            new_first[rows, :] = first_new
            new_second[rows, :] = second_new
            new_outer[rows, :] = outer_new
            new_anchor[rows, :] = anchor_new
            new_master[rows, :] = 0.5 * inner + 0.5 * anchor_new

    def do_send(p, s, at):
        for kind in range(len(links_of(GATHER[p][3][s]))):
            gather_copy(p, s, at, kind).start()

    def do_pass(p, s, at):
        gather_copy(p, s, at, 2).start()
        gather_copy(p, s, at, 3).start()

    def do_product(slot):
        for rows in (slice(0, 256), slice(256, 512)):
            value = jnp.dot(ref["grad"][rows, :], ref["weight"][tuple(SHARDS[slot].values())], preferred_element_type=F32)
            out_ref[rows, columns_of(SHARDS[slot])] = value.astype(BF16)

    def do_sum(k):
        if k == 1:
            ref["sum_send"][...] = ref["mast"][mine, :] + ref["sum_recv"][0]
        if k == 2:
            ref["sum"][mine, :] = ref["sum_send"][...] + ref["sum_recv"][1]
        if k < 3:
            sum_copy(k).start()

    steps = {
        "dot": do_dot,
        "far": do_far,
        "near": do_near,
        "final": do_final,
        "update": do_update,
        "send": do_send,
        "pass": do_pass,
        "product": do_product,
        "sum": do_sum,
    }

    mast_copy.wait()
    for copy in row_copies:
        copy.start()
    ref["weight"][0, 0, 0] = jnp.transpose(ref["mast"][...]).astype(BF16)
    pl.semaphore_wait(barrier, len(to))

    row_order = (2, 1, 3, 0)
    loaded = set()
    for name, needs, _, _, _ in in_order(make_tasks()):
        if name[0] == "dot":
            if not loaded:
                grad_copy.wait()
                ref["grad_t"][...] = jnp.transpose(ref["grad"][...].astype(F32)).astype(BF16)
            y = SHARDS[name[1]]["y"]
            if y not in loaded:
                loaded.add(y)
                row_copies[row_order.index(y)].wait()
                if len(loaded) == 4:
                    for copy in state_copies:
                        copy.start()
        for token in needs:
            wait_for(token)
        with jax.named_scope(name[0]):
            steps[name[0]](*name[1:])

    for p in range(len(REDUCE)):
        for sem in (ref[f"rs{p}"], ref[f"gs{p}"]):
            remote(ref[f"send{p}"], ref[f"recv{p}"], sem, sem, to["z"]).wait_send()
    for k in range(3):
        sum_copy(k).wait_send()


def write_out(*refs):
    count = len(refs) // 2
    sem = refs[-1]
    copies = []
    for k in range(count):
        src, dst = refs[k], refs[count + k]
        cuts = 8 if k == 0 else 1
        rows = src.shape[0] // cuts
        for c in range(cuts):
            part = pl.ds(c * rows, rows)
            copies.append(pltpu.make_async_copy(src.at[part], dst.at[part], sem.at[len(copies)]))
    for copy in copies:
        copy.start()
    for copy in copies:
        copy.wait()


def exchange(*args):
    own = layout()
    shapes = [((TOK, 32 * SHARD), BF16)] + [((SHARD, COLS), F32)] * 5
    results = pl.pallas_call(
        functools.partial(kernel, tuple(own.names)),
        out_shape=[pltpu.VMEM(*shape) for shape in shapes],
        in_specs=[pl.BlockSpec(memory_space=pltpu.HBM)] * 7,
        out_specs=[pl.BlockSpec(memory_space=pltpu.VMEM)] * 6,
        scratch_shapes=own.shapes,
        compiler_params=pltpu.CompilerParams(collective_id=0, has_side_effects=True, vmem_limit_bytes=53 << 20),
        cost_estimate=pl.CostEstimate(flops=2 * 2 * TOK * COLS * 32 * SHARD, bytes_accessed=20 << 20, transcendentals=0),
    )(*args)
    return pl.pallas_call(
        write_out,
        out_shape=[jax.ShapeDtypeStruct(*shape) for shape in shapes],
        in_specs=[pl.BlockSpec(memory_space=pltpu.VMEM)] * 6,
        out_specs=[pl.BlockSpec(memory_space=pltpu.HBM)] * 6,
        scratch_shapes=[pltpu.SemaphoreType.DMA((13,))],
        compiler_params=pltpu.CompilerParams(vmem_limit_bytes=4 << 20),
    )(*[pltpu.with_memory_space_constraint(r, pltpu.VMEM) for r in results])


def on_device(layer_input, out_grad, master, first_moment, second_moment, anchor, outer_moment):
    input_grad, master_new, first_new, second_new, anchor_new, outer_new = exchange(
        layer_input, out_grad, master[0], first_moment[0], second_moment[0], anchor, outer_moment
    )
    return (input_grad, master_new[None], first_new[None], second_new[None], anchor_new, outer_new)


def solution(mesh):
    return jax.shard_map(
        on_device,
        mesh=mesh,
        in_specs=(
            P(("rep", "fsdp"), None),
            P(("rep", "fsdp"), None),
            P("rep", "fsdp", None),
            P("rep", "fsdp", None),
            P("rep", "fsdp", None),
            P("fsdp", None),
            P("fsdp", None),
        ),
        out_specs=(
            P(("rep", "fsdp"), None),
            P("rep", "fsdp", None),
            P("rep", "fsdp", None),
            P("rep", "fsdp", None),
            P("fsdp", None),
            P("fsdp", None),
        ),
        check_vma=False,
    )
```
